32 devices in a mesh: member: 4 (over z), band: 8 (over y, x, core).
Axes of the slice: x: 2, y: 2, z: 4, core: 2. Of those that a mesh axis runs over, the one named last changes fastest.
Arguments:
- latent: bfloat16 [4, 2048, 1024], P('member', 'band'), may hold values from -6 to 6
- observed: bfloat16 [2048, 128], P('band'), may hold values from -6 to 6
- area_weight: float32 [2048], P('band'), may hold values from 0.3 to 25, as said below
- band_counts: int32 [8], replicated, may hold values from 128 to 256, as said below
- gain_attn: float32 [1024], replicated, may hold values from 0.25 to 1.75
- w_query: bfloat16 [1024, 1024], replicated, may hold values from -0.1875 to 0.1875
- w_key: bfloat16 [1024, 1024], replicated, may hold values from -0.1875 to 0.1875
- w_value: bfloat16 [1024, 1024], replicated, may hold values from -0.1875 to 0.1875
- w_out: bfloat16 [1024, 1024], replicated, may hold values from -1.5 to 1.5
- gain_head: float32 [1024], replicated, may hold values from 0.25 to 1.75
- w_head: bfloat16 [1024, 128], replicated, may hold values from -0.1875 to 0.1875
Outputs:
- grad_latent: bfloat16 [4, 2048, 1024], P('member', 'band')
- grad_head: float32 [1024, 128], P('band')
- ensemble_loss: float32 [], replicated
The draws below stay inside these ranges and needn't reach their ends.
Inputs may be any that keep to these rules, and one draw needn't show every extreme that they name: Band b holds band_counts[b] live grid points in its first slots; the remaining of its 256 slots are padding. In every draw some band holds exactly 256 and another exactly 128. `area_weight`: positive area weights.
All inputs are finite; a program needn't handle non-finite values.
Results may differ from the reference program's by a relative error of at most 0.019.
Values may be sent and summed in bfloat16 or wider, within the bound.
A program may use at most 192 MiB of HBM per device.

```python
import math
import jax
import jax.numpy as jnp
from jax import lax

D = 1024
HEADS = 16
CH = 128
R = 512
CAP = 256
CMIN = 128
HOPS = 4
MEMBERS = 4
BANDS = 8
POINTS = 2048


def draw_band_counts(key, part):
    base_key = jax.random.fold_in(key, 11)
    first_key, order_key = jax.random.split(base_key)
    counts_drawn = jax.random.randint(first_key, (BANDS,), CMIN, CAP + 1)
    order_drawn = jax.random.permutation(order_key, BANDS)
    counts_drawn = counts_drawn.at[order_drawn[0]].set(CAP)
    counts_drawn = counts_drawn.at[order_drawn[1]].set(CMIN)
    return counts_drawn.astype(jnp.int32)


def draw_area_weight(key, part):
    noise_key = jax.random.fold_in(key, 23)
    band_place = (jnp.arange(POINTS) // CAP).astype(jnp.float32) / (BANDS - 1)
    rising = jnp.log(3.0)
    spread = 0.7
    rough = jax.random.uniform(noise_key, (POINTS,), jnp.float32, -spread, spread)
    return jnp.exp(rising * band_place + rough).astype(jnp.float32)


def level_of(rng, dims, pieces, least, top_value):
    def one(dim, shards_of):
        draws = jax.random.uniform(jax.random.fold_in(jax.random.fold_in(rng, 6), dim), (shards_of,), jnp.float32, least / len(pieces), top_value / len(pieces))
        return jnp.repeat(jnp.exp(draws), dims[dim] // shards_of).reshape((-1,) + (1,) * (len(dims) - dim - 1))

    factor_of = one(*pieces[0])
    for cut in pieces[1:]:
        factor_of = factor_of * one(*cut)
    return factor_of


def noise(own_key, shape, scale, most, shards=(), kind=jnp.bfloat16):
    values = scale * jax.random.normal(own_key, shape, jnp.float32)
    if shards:
        values = values * level_of(own_key, shape, shards, -0.22, 0.18)
    return jnp.clip(values, -most, most).astype(kind)


def setup_inputs(seed: int = 0) -> dict:
    key_list = jax.random.split(jax.random.key(seed), 12)
    latent = noise(key_list[0], (MEMBERS, POINTS, D), 1.0, 6.0, ((0, 4), (1, 8)))
    observed = noise(key_list[1], (POINTS, CH), 1.0, 6.0, ((0, 8),))
    area_weight = draw_area_weight(jax.random.fold_in(key_list[11], 71), 0)
    band_counts = draw_band_counts(jax.random.fold_in(key_list[11], 71), 0)
    gain_attn = jnp.clip(1.0 + 0.15 * jax.random.normal(key_list[4], (D,), jnp.float32), 0.25, 1.75)
    w_query = noise(key_list[5], (D, D), D ** -0.5, 0.1875)
    w_key = noise(key_list[6], (D, D), D ** -0.5, 0.1875)
    w_value = noise(key_list[7], (D, D), D ** -0.5, 0.1875)
    w_out = noise(key_list[8], (D, D), (D // 64) ** -0.5, 1.5)
    gain_head = jnp.clip(1.0 + 0.15 * jax.random.normal(key_list[9], (D,), jnp.float32), 0.25, 1.75)
    w_head = noise(key_list[10], (D, CH), D ** -0.5, 0.1875)
    return dict(latent=latent, observed=observed, area_weight=area_weight, band_counts=band_counts, gain_attn=gain_attn, w_query=w_query, w_key=w_key, w_value=w_value, w_out=w_out, gain_head=gain_head, w_head=w_head)


NORM_EPS = 1e-06
SMOOTH_WIDTH = 0.25
FAIR_ALPHA = 0.95
heads_per_group = 4

def inverse_rms(values):
    return lax.rsqrt(lax.optimization_barrier(jnp.mean(values * values, axis=-1, keepdims=True)) + NORM_EPS)

def norm_backward(values, gain_vec, inverse, upstream):
    scaled = upstream * gain_vec
    return inverse * scaled - values * inverse ** 3 * lax.optimization_barrier(jnp.mean(values * scaled, axis=-1, keepdims=True))

def times_transposed(left_side, scaling_coefficient):
    return lax.dot_general(left_side, scaling_coefficient, (((left_side.ndim - 1,), (1,)), ((), ())), preferred_element_type=jnp.float32)

def window_probs(query_group, key_group, allowed):
    head_size = query_group.shape[-1]
    scores = jnp.einsum('mqgd,mkgd->mgqk', query_group.astype(jnp.float32), key_group.astype(jnp.float32)) / math.sqrt(head_size)
    exponent = jnp.where(allowed[None, None], jnp.exp(scores), 0.0)
    return exponent / lax.optimization_barrier(jnp.sum(exponent, axis=-1, keepdims=True))

def split_group(array_in, first_col, group_width, head_size):
    part_cols = lax.dynamic_slice_in_dim(array_in, first_col, group_width, 2)
    return part_cols.reshape(array_in.shape[0], array_in.shape[1], heads_per_group, head_size)

def attention_forward(queries, key_rows, value_rows, allowed):
    number_of_realizations, row_count, model_width = queries.shape
    head_size = model_width // HEADS
    group_width = heads_per_group * head_size

    def one_group(group_index, output):
        first_col = (group_index * group_width).astype(jnp.int32)
        query_group = split_group(queries, first_col, group_width, head_size)
        key_group = split_group(key_rows, first_col, group_width, head_size)
        value_group = split_group(value_rows, first_col, group_width, head_size)
        soft_b = window_probs(query_group, key_group, allowed).astype(jnp.bfloat16)
        mixed_group = jnp.einsum('mgqk,mkgd->mqgd', soft_b.astype(jnp.float32), value_group.astype(jnp.float32))
        mixed_group = mixed_group.reshape(number_of_realizations, row_count, group_width).astype(jnp.bfloat16)
        return lax.dynamic_update_slice_in_dim(output, mixed_group, first_col, 2)
    return lax.fori_loop(0, model_width // group_width, one_group, jnp.zeros(queries.shape, jnp.bfloat16))

def attention_backward(queries, key_rows, value_rows, allowed, grad_mixed):
    number_of_realizations, row_count, model_width = queries.shape
    key_count = key_rows.shape[1]
    head_size = model_width // HEADS
    group_width = heads_per_group * head_size
    score_scale = 1.0 / math.sqrt(head_size)

    def one_group(group_index, carried):
        grad_query, grad_key, grad_value = carried
        first_col = (group_index * group_width).astype(jnp.int32)
        query_group = split_group(queries, first_col, group_width, head_size)
        key_group = split_group(key_rows, first_col, group_width, head_size)
        value_group = split_group(value_rows, first_col, group_width, head_size)
        upstream_group = split_group(grad_mixed, first_col, group_width, head_size)
        soft = window_probs(query_group, key_group, allowed)
        soft_b = soft.astype(jnp.bfloat16)
        d_soft = jnp.einsum('mqgd,mkgd->mgqk', upstream_group.astype(jnp.float32), value_group.astype(jnp.float32))
        inner_sum = lax.optimization_barrier(jnp.sum(soft * d_soft, axis=-1, keepdims=True))
        d_score = (soft * (d_soft - inner_sum) * score_scale).astype(jnp.bfloat16)
        query_part = jnp.einsum('mgqk,mkgd->mqgd', d_score.astype(jnp.float32), key_group.astype(jnp.float32))
        key_part = jnp.einsum('mgqk,mqgd->mkgd', d_score.astype(jnp.float32), query_group.astype(jnp.float32))
        value_part = jnp.einsum('mgqk,mqgd->mkgd', soft_b.astype(jnp.float32), upstream_group.astype(jnp.float32))
        grad_query = lax.dynamic_update_slice_in_dim(grad_query, query_part.reshape(number_of_realizations, row_count, group_width).astype(jnp.bfloat16), first_col, 2)
        grad_key = lax.dynamic_update_slice_in_dim(grad_key, key_part.reshape(number_of_realizations, key_count, group_width).astype(jnp.bfloat16), first_col, 2)
        grad_value = lax.dynamic_update_slice_in_dim(grad_value, value_part.reshape(number_of_realizations, key_count, group_width).astype(jnp.bfloat16), first_col, 2)
        return (grad_query, grad_key, grad_value)
    initial = (jnp.zeros(queries.shape, jnp.bfloat16), jnp.zeros(key_rows.shape, jnp.bfloat16), jnp.zeros(value_rows.shape, jnp.bfloat16))
    return lax.fori_loop(0, model_width // group_width, one_group, initial)

def probabilistic_accuracy(predicted_states, measured_part, scaling_coefficient):
    number_of_realizations = predicted_states.shape[0]
    fair_factor = 1.0 - (1.0 - FAIR_ALPHA) / number_of_realizations
    gap_from_measured = predicted_states - measured_part[None]
    smooth_observed = jnp.sqrt(gap_from_measured * gap_from_measured + SMOOTH_WIDTH * SMOOTH_WIDTH)
    between_realization_gap = predicted_states[:, None] - predicted_states[None, :]
    smooth_pair = jnp.sqrt(between_realization_gap * between_realization_gap + SMOOTH_WIDTH * SMOOTH_WIDTH)
    off_diagonal = (1.0 - jnp.eye(number_of_realizations, dtype=jnp.float32))[:, :, None, None]
    point_score = lax.optimization_barrier(jnp.sum(smooth_observed, axis=0)) / number_of_realizations - fair_factor / (2.0 * number_of_realizations * (number_of_realizations - 1)) * lax.optimization_barrier(jnp.sum(off_diagonal * smooth_pair, axis=(0, 1)))
    total = jnp.sum(scaling_coefficient[:, None] * point_score)
    gradient = scaling_coefficient[None, :, None] * (gap_from_measured / smooth_observed / number_of_realizations - fair_factor / (number_of_realizations * (number_of_realizations - 1.0)) * lax.optimization_barrier(jnp.sum(between_realization_gap / smooth_pair, axis=1)))
    return (total, gradient)

def reference(latent, observed, area_weight, band_counts, gain_attn, w_query, w_key, w_value, w_out, gain_head, w_head):
    number_of_realizations = latent.shape[0]
    window_rows = (2 * HOPS + 1) * CAP
    pad_rows = HOPS * CAP
    slot_iota = jnp.arange(CAP, dtype=jnp.int32)
    offsets = (jnp.cumsum(band_counts) - band_counts).astype(jnp.int32)
    positions = (offsets[:, None] + slot_iota[None, :]).reshape(-1).astype(jnp.int32)
    live = (slot_iota[None, :] < band_counts[:, None]).reshape(-1)
    pos_pad = jnp.concatenate([jnp.zeros((pad_rows,), jnp.int32), positions, jnp.zeros((pad_rows,), jnp.int32)])
    live_pad = jnp.concatenate([jnp.zeros((pad_rows,), bool), live, jnp.zeros((pad_rows,), bool)])
    latent_f = latent.astype(jnp.float32)
    inverse_one = inverse_rms(latent_f)
    normed = (latent_f * inverse_one * gain_attn).astype(jnp.bfloat16)
    queries = jnp.dot(normed, w_query, preferred_element_type=jnp.float32).astype(jnp.bfloat16)
    key_rows = jnp.dot(normed, w_key, preferred_element_type=jnp.float32).astype(jnp.bfloat16)
    value_rows = jnp.dot(normed, w_value, preferred_element_type=jnp.float32).astype(jnp.bfloat16)
    zero_pad = jnp.zeros((number_of_realizations, pad_rows, D), jnp.bfloat16)
    key_pad = jnp.concatenate([zero_pad, key_rows, zero_pad], axis=1)
    value_pad = jnp.concatenate([zero_pad, value_rows, zero_pad], axis=1)

    def band_window(band_index):
        first_row = (band_index * CAP).astype(jnp.int32)
        query_block = lax.dynamic_slice_in_dim(queries, first_row, CAP, 1)
        key_block = lax.dynamic_slice_in_dim(key_pad, first_row, window_rows, 1)
        value_block = lax.dynamic_slice_in_dim(value_pad, first_row, window_rows, 1)
        query_pos = lax.dynamic_slice_in_dim(positions, first_row, CAP, 0)
        key_pos = lax.dynamic_slice_in_dim(pos_pad, first_row, window_rows, 0)
        key_live = lax.dynamic_slice_in_dim(live_pad, first_row, window_rows, 0)
        allowed = key_live[None, :] & (jnp.abs(query_pos[:, None] - key_pos[None, :]) <= R)
        return (first_row, query_block, key_block, value_block, allowed)

    def band_forward(band_index):
        window = band_window(band_index)
        return attention_forward(window[1], window[2], window[3], window[4])
    band_list = jnp.arange(BANDS, dtype=jnp.int32)
    mixed_blocks = lax.map(band_forward, band_list)
    mixed_out = jnp.transpose(mixed_blocks, (1, 0, 2, 3)).reshape(number_of_realizations, POINTS, D)
    hidden = latent_f + jnp.dot(mixed_out, w_out, preferred_element_type=jnp.float32)
    inverse_two = inverse_rms(hidden)
    head_in = (hidden * inverse_two * gain_head).astype(jnp.bfloat16)
    predicted = jnp.dot(head_in, w_head, preferred_element_type=jnp.float32).astype(jnp.bfloat16)
    point_weight = area_weight * live.astype(jnp.float32) / (jnp.sum(band_counts).astype(jnp.float32) * CH)
    ensemble_loss, gradient = probabilistic_accuracy(predicted.astype(jnp.float32), observed.astype(jnp.float32), point_weight)
    grad_pred = gradient.astype(jnp.bfloat16)
    grad_head = lax.dot_general(head_in.reshape(-1, D), grad_pred.reshape(-1, CH), (((0,), (0,)), ((), ())), preferred_element_type=jnp.float32)
    grad_hidden = norm_backward(hidden, gain_head, inverse_two, times_transposed(grad_pred, w_head))
    grad_mixed = times_transposed(grad_hidden.astype(jnp.bfloat16), w_out).astype(jnp.bfloat16)

    def band_backward(normed_acc, band_index):
        window = band_window(band_index)
        first_row = window[0]
        upstream = lax.dynamic_slice_in_dim(grad_mixed, first_row, CAP, 1)
        grad_query, key_term, value_term = attention_backward(window[1], window[2], window[3], window[4], upstream)
        normed_term = (times_transposed(key_term, w_key) + times_transposed(value_term, w_value)).astype(jnp.bfloat16)
        normed_sum = lax.dynamic_slice_in_dim(normed_acc, first_row, window_rows, 1) + normed_term.astype(jnp.float32)
        normed_acc = lax.dynamic_update_slice_in_dim(normed_acc, normed_sum, first_row, 1)
        return (normed_acc, grad_query)
    acc_zero = jnp.zeros((number_of_realizations, POINTS + 2 * pad_rows, D), jnp.float32)
    normed_acc, query_blocks = lax.scan(band_backward, acc_zero, band_list)
    grad_queries = jnp.transpose(query_blocks, (1, 0, 2, 3)).reshape(number_of_realizations, POINTS, D)
    grad_normed = times_transposed(grad_queries, w_query) + normed_acc[:, pad_rows:pad_rows + POINTS]
    grad_latent = (grad_hidden + norm_backward(latent_f, gain_attn, inverse_one, grad_normed)).astype(jnp.bfloat16)
    return (grad_latent, grad_head, ensemble_loss)
```

```python
import functools
import math

import jax
import jax.numpy as jnp
from jax import lax
from jax.experimental import pallas as pl
from jax.experimental.pallas import tpu as pltpu
from jax.sharding import PartitionSpec as P

HEADS = 16
CH = 128
R = 512
HOPS = 4


NORM_EPS = 1e-06
SMOOTH_WIDTH = 0.25
FAIR_ALPHA = 0.95
LANES = 128
MASKED = -1e30
VMEM_BYTES = 56 * 1024 * 1024


def inverse_rms(values):
    return lax.rsqrt(jnp.mean(values * values, axis=-1, keepdims=True) + NORM_EPS)


def norm_backward(values, gain_vec, inverse, upstream):
    scaled = upstream * gain_vec
    return inverse * scaled - values * inverse**3 * jnp.mean(
        values * scaled, axis=-1, keepdims=True
    )


def times_transposed(left_side, scaling_coefficient):
    return lax.dot_general(
        left_side,
        scaling_coefficient,
        (((left_side.ndim - 1,), (1,)), ((), ())),
        preferred_element_type=jnp.float32,
    )


def dot_last(left_side, right_side):
    return lax.dot_general(
        left_side, right_side, (((1,), (1,)), ((), ())), preferred_element_type=jnp.float32
    )


def dot_first(left_side, right_side):
    return lax.dot_general(
        left_side, right_side, (((0,), (0,)), ((), ())), preferred_element_type=jnp.float32
    )


def head_masks(shape, dimension, heads, head_size):
    lane = lax.broadcasted_iota(jnp.int32, shape, dimension)
    return [(lane >= h * head_size) & (lane < (h + 1) * head_size) for h in range(heads)]


def masked_heads(block, masks, factor):
    wide = block.astype(jnp.float32) * factor
    return [jnp.where(mask, wide, 0.0).astype(jnp.bfloat16) for mask in masks]


def forward_kernel(
    head_size, tile, reach_ref, q_ref, k_ref, v_ref, bias_ref, out_ref, lse_ref, exp_ref
):
    heads = LANES // head_size
    rows = q_ref.shape[0]
    scale = 1.0 / math.sqrt(head_size)
    masks = head_masks(q_ref.shape, 1, heads, head_size)
    query_heads = masked_heads(q_ref[...], masks, scale)

    def score_step(block, totals):
        at = pl.ds(pl.multiple_of(block * tile, tile), tile)
        keys = k_ref[at, :]
        bias = bias_ref[at, :]
        new = []
        for h in range(heads):
            weight = jnp.exp(dot_last(keys, query_heads[h]) + bias)
            exp_ref[h, at, :] = weight
            new.append(totals[h] + jnp.sum(weight.reshape(tile // 8, 8, rows), axis=0))
        return tuple(new)

    zero = tuple(jnp.zeros((8, rows), jnp.float32) for _ in range(heads))
    partial = lax.fori_loop(reach_ref[0], reach_ref[1], score_step, zero)
    totals = [jnp.sum(part, axis=0, keepdims=True) for part in partial]
    shrink = [jnp.where(total > 1e30, 0.0625, 1.0) for total in totals]
    inverse = [1.0 / (total * small) for total, small in zip(totals, shrink)]

    def value_step(block, mixed):
        at = pl.ds(pl.multiple_of(block * tile, tile), tile)
        values = v_ref[at, :]
        return tuple(
            mixed[h] + dot_first(values, (exp_ref[h, at, :] * inverse[h]).astype(jnp.bfloat16))
            for h in range(heads)
        )

    zero = tuple(jnp.zeros((LANES, rows), jnp.float32) for _ in range(heads))
    mixed = lax.fori_loop(reach_ref[0], reach_ref[1], value_step, zero)
    columns = jnp.concatenate(
        [mixed[h][h * head_size : (h + 1) * head_size] * shrink[h] for h in range(heads)], axis=0
    )
    out_ref[...] = columns.T
    for h in range(heads):
        lse_ref[0, h : h + 1, :] = jnp.log(totals[h])


def backward_kernel(
    head_size,
    tile,
    reach_ref,
    q_ref,
    k_ref,
    v_ref,
    up_ref,
    mixed_ref,
    lse_ref,
    bias_ref,
    dq_ref,
    dk_ref,
    dv_ref,
):
    heads = LANES // head_size
    rows = q_ref.shape[0]
    scale = 1.0 / math.sqrt(head_size)
    masks = head_masks(q_ref.shape, 1, heads, head_size)
    query_heads = masked_heads(q_ref[...], masks, scale)
    up_heads = masked_heads(up_ref[...], masks, 1.0)
    product = (up_ref[...].astype(jnp.float32) * mixed_ref[...]).T
    inner = [
        jnp.sum(product[h * head_size : (h + 1) * head_size], axis=0, keepdims=True)
        for h in range(heads)
    ]
    lse = [lse_ref[0, h : h + 1, :] for h in range(heads)]

    def clear(block, carry):
        at = pl.ds(pl.multiple_of(block * tile, tile), tile)
        dk_ref[at, :] = jnp.zeros((tile, LANES), jnp.bfloat16)
        dv_ref[at, :] = jnp.zeros((tile, LANES), jnp.bfloat16)
        return carry

    lax.fori_loop(0, reach_ref[0], clear, 0)
    lax.fori_loop(reach_ref[1], k_ref.shape[0] // tile, clear, 0)

    def step(block, grads):
        at = pl.ds(pl.multiple_of(block * tile, tile), tile)
        keys = k_ref[at, :]
        values = v_ref[at, :]
        bias = bias_ref[at, :]
        key_sum = jnp.zeros((tile, LANES), jnp.float32)
        value_sum = jnp.zeros((tile, LANES), jnp.float32)
        new = []
        for h in range(heads):
            soft = jnp.exp(dot_last(keys, query_heads[h]) + (bias - lse[h]))
            d_soft = dot_last(values, up_heads[h])
            d_score = (soft * (d_soft - inner[h])).astype(jnp.bfloat16)
            key_sum += jnp.dot(d_score, query_heads[h], preferred_element_type=jnp.float32)
            value_sum += jnp.dot(
                soft.astype(jnp.bfloat16), up_heads[h], preferred_element_type=jnp.float32
            )
            new.append(grads[h] + dot_first(keys, d_score))
        dk_ref[at, :] = key_sum.astype(jnp.bfloat16)
        dv_ref[at, :] = value_sum.astype(jnp.bfloat16)
        return tuple(new)

    zero = tuple(jnp.zeros((LANES, rows), jnp.float32) for _ in range(heads))
    grads = lax.fori_loop(reach_ref[0], reach_ref[1], step, zero)
    columns = jnp.concatenate(
        [grads[h][h * head_size : (h + 1) * head_size] for h in range(heads)], axis=0
    )
    dq_ref[...] = (columns * scale).T.astype(jnp.bfloat16)


def attention_forward(queries, key_rows, value_rows, bias, reach):
    rows, model_width = queries.shape
    slots = key_rows.shape[0]
    head_size = model_width // HEADS
    heads = LANES // head_size
    steps = model_width // LANES
    return pl.pallas_call(
        functools.partial(forward_kernel, head_size, rows),
        grid=(steps,),
        in_specs=[
            pl.BlockSpec(memory_space=pltpu.SMEM),
            pl.BlockSpec((rows, LANES), lambda i: (0, i)),
            pl.BlockSpec((slots, LANES), lambda i: (0, i)),
            pl.BlockSpec((slots, LANES), lambda i: (0, i)),
            pl.BlockSpec((slots, rows), lambda i: (0, 0)),
        ],
        out_specs=[
            pl.BlockSpec((rows, LANES), lambda i: (0, i)),
            pl.BlockSpec((1, heads, rows), lambda i: (i, 0, 0)),
        ],
        out_shape=[
            jax.ShapeDtypeStruct((rows, model_width), jnp.float32),
            jax.ShapeDtypeStruct((steps, heads, rows), jnp.float32),
        ],
        scratch_shapes=[pltpu.VMEM((heads, slots, rows), jnp.float32)],
        compiler_params=pltpu.CompilerParams(vmem_limit_bytes=VMEM_BYTES),
        name="attention_forward",
    )(reach, queries, key_rows, value_rows, bias)


def attention_backward(queries, key_rows, value_rows, upstream, mixed, lse, bias, reach):
    rows, model_width = queries.shape
    slots = key_rows.shape[0]
    head_size = model_width // HEADS
    heads = LANES // head_size
    row_spec = pl.BlockSpec((rows, LANES), lambda i: (0, i))
    slot_spec = pl.BlockSpec((slots, LANES), lambda i: (0, i))
    return pl.pallas_call(
        functools.partial(backward_kernel, head_size, rows),
        grid=(model_width // LANES,),
        in_specs=[
            pl.BlockSpec(memory_space=pltpu.SMEM),
            row_spec,
            slot_spec,
            slot_spec,
            row_spec,
            row_spec,
            pl.BlockSpec((1, heads, rows), lambda i: (i, 0, 0)),
            pl.BlockSpec((slots, rows), lambda i: (0, 0)),
        ],
        out_specs=[row_spec, slot_spec, slot_spec],
        out_shape=[
            jax.ShapeDtypeStruct((rows, model_width), jnp.bfloat16),
            jax.ShapeDtypeStruct((slots, model_width), jnp.bfloat16),
            jax.ShapeDtypeStruct((slots, model_width), jnp.bfloat16),
        ],
        compiler_params=pltpu.CompilerParams(vmem_limit_bytes=VMEM_BYTES),
        name="attention_backward",
    )(reach, queries, key_rows, value_rows, upstream, mixed, lse, bias)


def own_accuracy(own, everyone, member, measured, weight):
    members = everyone.shape[0]
    fair = 1.0 - (1.0 - FAIR_ALPHA) / members
    gap = own - measured
    smooth = jnp.sqrt(gap * gap + SMOOTH_WIDTH * SMOOTH_WIDTH)
    pair_sum = jnp.zeros_like(gap)
    slope_sum = jnp.zeros_like(gap)
    for other in range(members):
        pair_gap = own - everyone[other]
        pair = jnp.sqrt(pair_gap * pair_gap + SMOOTH_WIDTH * SMOOTH_WIDTH)
        pair_sum += jnp.where(member == other, 0.0, pair)
        slope_sum += pair_gap / pair
    score = smooth / members - fair / (2.0 * members * (members - 1)) * pair_sum
    gradient = weight * (gap / smooth / members - fair / (members * (members - 1.0)) * slope_sum)
    return jnp.sum(weight * score), gradient


def body(
    latent,
    observed,
    area_weight,
    band_counts,
    gain_attn,
    w_query,
    w_key,
    w_value,
    w_out,
    gain_head,
    w_head,
):
    band = lax.axis_index("band")
    bands = lax.axis_size("band")
    member = lax.axis_index("member")
    _, slots, model_width = latent.shape
    channels = w_head.shape[1]
    window = min(bands, 2 * HOPS + 1)
    first_band = jnp.clip(band - HOPS, 0, bands - window)

    latent_f = latent[0].astype(jnp.float32)
    inverse_one = inverse_rms(latent_f)
    normed = (latent_f * inverse_one * gain_attn).astype(jnp.bfloat16)
    gathered = lax.all_gather(normed, "band", axis=0, tiled=True)
    normed_rows = lax.dynamic_slice_in_dim(gathered, first_band * slots, window * slots, 0)
    queries = jnp.dot(normed, w_query, preferred_element_type=jnp.float32).astype(jnp.bfloat16)

    slot_iota = jnp.arange(slots, dtype=jnp.int32)
    offsets = jnp.cumsum(band_counts) - band_counts
    own_first = offsets[band]
    own_pos = own_first + slot_iota
    own_live = slot_iota < band_counts[band]
    near = first_band + jnp.arange(window, dtype=jnp.int32)
    near_first = lax.dynamic_slice_in_dim(offsets, first_band, window, 0)
    near_count = lax.dynamic_slice_in_dim(band_counts, first_band, window, 0)
    within = jnp.abs(near - band) <= HOPS
    key_pos = near_first[:, None] + slot_iota[None, :]
    key_live = (slot_iota[None, :] < near_count[:, None]) & within[:, None]
    key_pos = key_pos.reshape(-1)
    allowed = key_live.reshape(-1)[:, None] & (jnp.abs(key_pos[:, None] - own_pos[None, :]) <= R)
    bias = jnp.where(allowed, 0.0, MASKED).astype(jnp.float32)
    reached = (
        within
        & (near_first <= own_first + (slots - 1) + R)
        & (near_first + near_count - 1 >= own_first - R)
    )
    index = jnp.arange(window, dtype=jnp.int32)
    reach = jnp.stack(
        [
            jnp.min(jnp.where(reached, index, window)),
            jnp.max(jnp.where(reached, index + 1, 0)),
        ]
    ).astype(jnp.int32)

    key_rows = jnp.dot(normed_rows, w_key, preferred_element_type=jnp.float32).astype(jnp.bfloat16)
    value_rows = jnp.dot(normed_rows, w_value, preferred_element_type=jnp.float32).astype(
        jnp.bfloat16
    )
    mixed, lse = attention_forward(queries, key_rows, value_rows, bias, reach)
    hidden = latent_f + jnp.dot(
        mixed.astype(jnp.bfloat16), w_out, preferred_element_type=jnp.float32
    )
    inverse_two = inverse_rms(hidden)
    head_in = (hidden * inverse_two * gain_head).astype(jnp.bfloat16)
    predicted = jnp.dot(head_in, w_head, preferred_element_type=jnp.float32).astype(jnp.bfloat16)
    everyone = lax.all_gather(predicted, "member", axis=0, tiled=False)
    total_live = jnp.sum(band_counts).astype(jnp.float32) * CH
    point_weight = area_weight * own_live.astype(jnp.float32) / total_live
    loss_part, gradient = own_accuracy(
        predicted.astype(jnp.float32),
        everyone.astype(jnp.float32),
        member,
        observed.astype(jnp.float32),
        point_weight[:, None],
    )
    grad_pred = gradient.astype(jnp.bfloat16)
    grad_hidden = norm_backward(hidden, gain_head, inverse_two, times_transposed(grad_pred, w_head))
    grad_mixed = times_transposed(grad_hidden.astype(jnp.bfloat16), w_out).astype(jnp.bfloat16)

    head_part = dot_first(head_in, grad_pred).reshape(bands, model_width // bands, channels)
    loss_rows = jnp.broadcast_to(loss_part, (bands, 8, channels))
    packed = jnp.concatenate([head_part, loss_rows], axis=1)
    packed = lax.psum_scatter(packed, "band", scatter_dimension=0, tiled=False)
    packed = jnp.sum(lax.all_gather(packed, "member", axis=0, tiled=False), axis=0)
    grad_head = packed[: model_width // bands]
    ensemble_loss = packed[model_width // bands, 0]

    grad_queries, key_terms, value_terms = attention_backward(
        queries, key_rows, value_rows, grad_mixed, mixed, lse, bias, reach
    )
    terms = (times_transposed(key_terms, w_key) + times_transposed(value_terms, w_value)).astype(
        jnp.bfloat16
    )
    if window < bands:
        terms = lax.dynamic_update_slice_in_dim(
            jnp.zeros((bands * slots, model_width), jnp.bfloat16), terms, first_band * slots, 0
        )
    normed_total = lax.psum_scatter(terms, "band", scatter_dimension=0, tiled=True)
    grad_normed = times_transposed(grad_queries, w_query) + normed_total.astype(jnp.float32)
    grad_latent = (
        grad_hidden + norm_backward(latent_f, gain_attn, inverse_one, grad_normed)
    ).astype(jnp.bfloat16)
    return (grad_latent[None], grad_head, ensemble_loss)


def solution(mesh):
    placed = (
        P("member", "band", None),
        P("band", None),
        P("band"),
        P(),
        P(),
        P(),
        P(),
        P(),
        P(),
        P(),
        P(),
    )
    return jax.shard_map(
        body,
        mesh=mesh,
        in_specs=placed,
        out_specs=(P("member", "band", None), P("band", None), P()),
        check_vma=False,
    )
```

```python
import functools
import math

import jax
import jax.numpy as jnp
from jax import lax
from jax.experimental import pallas as pl
from jax.experimental.pallas import tpu as pltpu
from jax.sharding import PartitionSpec as P

HEADS = 16
CH = 128
R = 512
HOPS = 4


NORM_EPS = 1e-06
SMOOTH_WIDTH = 0.25
FAIR_ALPHA = 0.95
LANES = 128
MASKED = -1e30
VMEM_BYTES = 56 * 1024 * 1024


def inverse_rms(values):
    return lax.rsqrt(jnp.mean(values * values, axis=-1, keepdims=True) + NORM_EPS)


def norm_backward(values, gain_vec, inverse, upstream):
    scaled = upstream * gain_vec
    return inverse * scaled - values * inverse**3 * jnp.mean(
        values * scaled, axis=-1, keepdims=True
    )


def times_transposed(left_side, scaling_coefficient):
    return lax.dot_general(
        left_side,
        scaling_coefficient,
        (((left_side.ndim - 1,), (1,)), ((), ())),
        preferred_element_type=jnp.float32,
    )


def dot_last(left_side, right_side):
    return lax.dot_general(
        left_side, right_side, (((1,), (1,)), ((), ())), preferred_element_type=jnp.float32
    )


def dot_first(left_side, right_side):
    return lax.dot_general(
        left_side, right_side, (((0,), (0,)), ((), ())), preferred_element_type=jnp.float32
    )


def head_masks(shape, dimension, heads, head_size):
    lane = lax.broadcasted_iota(jnp.int32, shape, dimension)
    return [(lane >= h * head_size) & (lane < (h + 1) * head_size) for h in range(heads)]


def masked_heads(block, masks, factor):
    wide = block.astype(jnp.float32) * factor
    return [jnp.where(mask, wide, 0.0).astype(jnp.bfloat16) for mask in masks]


def forward_kernel(
    head_size, tile, reach_ref, q_ref, k_ref, v_ref, bias_ref, out_ref, lse_ref, exp_ref
):
    heads = LANES // head_size
    rows = q_ref.shape[0]
    scale = 1.0 / math.sqrt(head_size)
    masks = head_masks(q_ref.shape, 1, heads, head_size)
    query_heads = masked_heads(q_ref[...], masks, scale)

    def score_step(block, totals):
        at = pl.ds(pl.multiple_of(block * tile, tile), tile)
        keys = k_ref[at, :]
        bias = bias_ref[at, :]
        new = []
        for h in range(heads):
            weight = jnp.exp(dot_last(keys, query_heads[h]) + bias)
            exp_ref[h, at, :] = weight
            new.append(totals[h] + jnp.sum(weight.reshape(tile // 8, 8, rows), axis=0))
        return tuple(new)

    zero = tuple(jnp.zeros((8, rows), jnp.float32) for _ in range(heads))
    partial = lax.fori_loop(reach_ref[0], reach_ref[1], score_step, zero)
    totals = [jnp.sum(part, axis=0, keepdims=True) for part in partial]
    shrink = [jnp.where(total > 1e30, 0.0625, 1.0) for total in totals]
    inverse = [1.0 / (total * small) for total, small in zip(totals, shrink)]

    def value_step(block, mixed):
        at = pl.ds(pl.multiple_of(block * tile, tile), tile)
        values = v_ref[at, :]
        return tuple(
            mixed[h] + dot_first(values, (exp_ref[h, at, :] * inverse[h]).astype(jnp.bfloat16))
            for h in range(heads)
        )

    zero = tuple(jnp.zeros((LANES, rows), jnp.float32) for _ in range(heads))
    mixed = lax.fori_loop(reach_ref[0], reach_ref[1], value_step, zero)
    columns = jnp.concatenate(
        [mixed[h][h * head_size : (h + 1) * head_size] * shrink[h] for h in range(heads)], axis=0
    )
    out_ref[...] = columns.T
    for h in range(heads):
        lse_ref[0, h : h + 1, :] = jnp.log(totals[h])


def backward_kernel(
    head_size,
    tile,
    reach_ref,
    q_ref,
    k_ref,
    v_ref,
    up_ref,
    mixed_ref,
    lse_ref,
    bias_ref,
    dq_ref,
    dk_ref,
    dv_ref,
):
    heads = LANES // head_size
    rows = q_ref.shape[0]
    scale = 1.0 / math.sqrt(head_size)
    masks = head_masks(q_ref.shape, 1, heads, head_size)
    query_heads = masked_heads(q_ref[...], masks, scale)
    up_heads = masked_heads(up_ref[...], masks, 1.0)
    product = (up_ref[...].astype(jnp.float32) * mixed_ref[...]).T
    inner = [
        jnp.sum(product[h * head_size : (h + 1) * head_size], axis=0, keepdims=True)
        for h in range(heads)
    ]
    lse = [lse_ref[0, h : h + 1, :] for h in range(heads)]

    def clear(block, carry):
        at = pl.ds(pl.multiple_of(block * tile, tile), tile)
        dk_ref[at, :] = jnp.zeros((tile, LANES), jnp.bfloat16)
        dv_ref[at, :] = jnp.zeros((tile, LANES), jnp.bfloat16)
        return carry

    lax.fori_loop(0, reach_ref[0], clear, 0)
    lax.fori_loop(reach_ref[1], k_ref.shape[0] // tile, clear, 0)

    def step(block, grads):
        at = pl.ds(pl.multiple_of(block * tile, tile), tile)
        keys = k_ref[at, :]
        values = v_ref[at, :]
        bias = bias_ref[at, :]
        key_sum = jnp.zeros((tile, LANES), jnp.float32)
        value_sum = jnp.zeros((tile, LANES), jnp.float32)
        new = []
        for h in range(heads):
            soft = jnp.exp(dot_last(keys, query_heads[h]) + (bias - lse[h]))
            d_soft = dot_last(values, up_heads[h])
            d_score = (soft * (d_soft - inner[h])).astype(jnp.bfloat16)
            key_sum += jnp.dot(d_score, query_heads[h], preferred_element_type=jnp.float32)
            value_sum += jnp.dot(
                soft.astype(jnp.bfloat16), up_heads[h], preferred_element_type=jnp.float32
            )
            new.append(grads[h] + dot_first(keys, d_score))
        dk_ref[at, :] = key_sum.astype(jnp.bfloat16)
        dv_ref[at, :] = value_sum.astype(jnp.bfloat16)
        return tuple(new)

    zero = tuple(jnp.zeros((LANES, rows), jnp.float32) for _ in range(heads))
    grads = lax.fori_loop(reach_ref[0], reach_ref[1], step, zero)
    columns = jnp.concatenate(
        [grads[h][h * head_size : (h + 1) * head_size] for h in range(heads)], axis=0
    )
    dq_ref[...] = (columns * scale).T.astype(jnp.bfloat16)


def attention_forward(queries, key_rows, value_rows, bias, reach):
    rows, model_width = queries.shape
    slots = key_rows.shape[0]
    head_size = model_width // HEADS
    heads = LANES // head_size
    steps = model_width // LANES
    return pl.pallas_call(
        functools.partial(forward_kernel, head_size, rows),
        grid=(steps,),
        in_specs=[
            pl.BlockSpec(memory_space=pltpu.SMEM),
            pl.BlockSpec((rows, LANES), lambda i: (0, i)),
            pl.BlockSpec((slots, LANES), lambda i: (0, i)),
            pl.BlockSpec((slots, LANES), lambda i: (0, i)),
            pl.BlockSpec((slots, rows), lambda i: (0, 0)),
        ],
        out_specs=[
            pl.BlockSpec((rows, LANES), lambda i: (0, i)),
            pl.BlockSpec((1, heads, rows), lambda i: (i, 0, 0)),
        ],
        out_shape=[
            jax.ShapeDtypeStruct((rows, model_width), jnp.float32),
            jax.ShapeDtypeStruct((steps, heads, rows), jnp.float32),
        ],
        scratch_shapes=[pltpu.VMEM((heads, slots, rows), jnp.float32)],
        compiler_params=pltpu.CompilerParams(vmem_limit_bytes=VMEM_BYTES),
        name="attention_forward",
    )(reach, queries, key_rows, value_rows, bias)


def attention_backward(queries, key_rows, value_rows, upstream, mixed, lse, bias, reach):
    rows, model_width = queries.shape
    slots = key_rows.shape[0]
    head_size = model_width // HEADS
    heads = LANES // head_size
    row_spec = pl.BlockSpec((rows, LANES), lambda i: (0, i))
    slot_spec = pl.BlockSpec((slots, LANES), lambda i: (0, i))
    return pl.pallas_call(
        functools.partial(backward_kernel, head_size, rows),
        grid=(model_width // LANES,),
        in_specs=[
            pl.BlockSpec(memory_space=pltpu.SMEM),
            row_spec,
            slot_spec,
            slot_spec,
            row_spec,
            row_spec,
            pl.BlockSpec((1, heads, rows), lambda i: (i, 0, 0)),
            pl.BlockSpec((slots, rows), lambda i: (0, 0)),
        ],
        out_specs=[row_spec, slot_spec, slot_spec],
        out_shape=[
            jax.ShapeDtypeStruct((rows, model_width), jnp.bfloat16),
            jax.ShapeDtypeStruct((slots, model_width), jnp.bfloat16),
            jax.ShapeDtypeStruct((slots, model_width), jnp.bfloat16),
        ],
        compiler_params=pltpu.CompilerParams(vmem_limit_bytes=VMEM_BYTES),
        name="attention_backward",
    )(reach, queries, key_rows, value_rows, upstream, mixed, lse, bias)


MESH = pl.DeviceIdType.MESH
COLUMNS = 256


def partner(index, distance):
    bit = 1
    flipped = index
    while bit <= distance:
        if distance & bit:
            flipped = flipped + (1 - 2 * ((index // bit) % 2)) * bit
        bit *= 2
    return flipped


def band_layout():
    band = lax.axis_index("band")
    return lax.axis_index("member"), band, band // 2, band % 2


def far_first(pairs):
    return sorted(range(1, pairs), key=lambda d: (-bin(d).count("1"), d))


def greet(targets):
    barrier = pltpu.get_barrier_semaphore()
    for target in targets:
        pl.semaphore_signal(barrier, inc=1, device_id=target, device_id_type=MESH)
    pl.semaphore_wait(barrier, len(targets))


def send(source, target_ref, send_sem, recv_sem, target):
    return pltpu.make_async_remote_copy(
        src_ref=source,
        dst_ref=target_ref,
        send_sem=send_sem,
        recv_sem=recv_sem,
        device_id=target,
        device_id_type=MESH,
    )


def project_into(rows_ref, weight_ref, out_ref):
    @pl.loop(0, weight_ref.shape[1] // COLUMNS)
    def _(tile):
        at = pl.ds(pl.multiple_of(tile * COLUMNS, COLUMNS), COLUMNS)
        out_ref[:, at] = jnp.dot(
            rows_ref[...], weight_ref[:, at], preferred_element_type=jnp.float32
        ).astype(out_ref.dtype)


def gather_kernel(
    bands,
    window,
    normed_ref,
    wq_ref,
    wk_ref,
    wv_ref,
    q_ref,
    k_ref,
    v_ref,
    held,
    send_sem,
    recv_sem,
    pass_send,
    pass_recv,
):
    member, band, pair, core = band_layout()
    pairs = bands // 2
    slots = normed_ref.shape[0]
    sibling = (member, 2 * pair + 1 - core)
    order = far_first(pairs)
    targets = {d: (member, 2 * partner(pair, d) + core) for d in order}
    greet([sibling] + [targets[d] for d in order])
    copies = {
        d: send(normed_ref, held.at[band], send_sem.at[d], recv_sem.at[d], targets[d])
        for d in order
    }
    copies[0] = send(normed_ref, held.at[band], send_sem.at[0], recv_sem.at[0], sibling)
    for d in order + [0]:
        copies[d].start()
    first = jnp.clip(band - HOPS, 0, bands - window)

    def project(rows_ref, source):
        def run():
            place = pl.ds(pl.multiple_of((source - first) * slots, slots), slots)
            project_into(rows_ref, wk_ref, k_ref.at[place])
            project_into(rows_ref, wv_ref, v_ref.at[place])

        if window == bands:
            run()
        else:
            pl.when((source >= first) & (source < first + window))(run)

    project_into(normed_ref, wq_ref, q_ref)
    project(normed_ref, band)
    copies[0].wait_recv()
    project(held.at[2 * pair + 1 - core], 2 * pair + 1 - core)
    passes = {}
    near_first = order[::-1]
    for d in near_first:
        copies[d].wait_recv()
        source = 2 * partner(pair, d) + core
        passes[d] = send(
            held.at[source], held.at[source], pass_send.at[d], pass_recv.at[d], sibling
        )
        passes[d].start()
        project(held.at[source], source)
    for d in near_first:
        passes[d].wait_recv()
        source = 2 * partner(pair, d) + 1 - core
        project(held.at[source], source)
    for d in order + [0]:
        copies[d].wait_send()
    for d in order:
        passes[d].wait_send()


def gather_and_project(normed, w_query, w_key, w_value, bands, window):
    slots, model_width = normed.shape
    vmem = pl.BlockSpec(memory_space=pltpu.VMEM)
    pairs = bands // 2
    return pl.pallas_call(
        functools.partial(gather_kernel, bands, window),
        in_specs=[vmem] * 4,
        out_specs=[vmem] * 3,
        out_shape=[
            jax.ShapeDtypeStruct((slots, model_width), jnp.bfloat16),
            jax.ShapeDtypeStruct((window * slots, model_width), jnp.bfloat16),
            jax.ShapeDtypeStruct((window * slots, model_width), jnp.bfloat16),
        ],
        scratch_shapes=[
            pltpu.VMEM((bands, slots, model_width), jnp.bfloat16),
            pltpu.SemaphoreType.DMA((pairs,)),
            pltpu.SemaphoreType.DMA((pairs,)),
            pltpu.SemaphoreType.DMA((pairs,)),
            pltpu.SemaphoreType.DMA((pairs,)),
        ],
        compiler_params=pltpu.CompilerParams(
            collective_id=0, has_side_effects=True, vmem_limit_bytes=VMEM_BYTES
        ),
        name="gather_rows",
    )(normed, w_query, w_key, w_value)


def member_targets(members):
    member = lax.axis_index("member")
    band = lax.axis_index("band")
    return [(lax.rem(member + d, members), band) for d in range(1, members)]


def exchange_kernel(members, own_ref, all_ref, held, send_sem, recv_sem):
    targets = member_targets(members)
    greet(targets)
    copies = [
        send(own_ref, held.at[d], send_sem.at[d], recv_sem.at[d], targets[d])
        for d in range(members - 1)
    ]
    for copy in copies:
        copy.start()
    for d, copy in enumerate(copies):
        copy.wait_recv()
        all_ref[d] = held[d]
    for copy in copies:
        copy.wait_send()


def exchange_members(own, members):
    vmem = pl.BlockSpec(memory_space=pltpu.VMEM)
    return pl.pallas_call(
        functools.partial(exchange_kernel, members),
        in_specs=[vmem],
        out_specs=vmem,
        out_shape=jax.ShapeDtypeStruct((members - 1,) + own.shape, own.dtype),
        scratch_shapes=[
            pltpu.VMEM((members - 1,) + own.shape, own.dtype),
            pltpu.SemaphoreType.DMA((members - 1,)),
            pltpu.SemaphoreType.DMA((members - 1,)),
        ],
        compiler_params=pltpu.CompilerParams(collective_id=1, has_side_effects=True),
        name="exchange_members",
    )(own)


def terms_kernel(
    bands,
    members,
    window,
    dk_ref,
    dv_ref,
    wk_ref,
    wv_ref,
    head_ref,
    total_ref,
    head_out,
    for_sibling,
    from_sibling,
    outgoing,
    arriving,
    head_held,
    sib_send,
    sib_recv,
    far_send,
    far_recv,
    head_send,
    head_recv,
):
    member, band, pair, core = band_layout()
    pairs = bands // 2
    slots = total_ref.shape[0]
    sibling = (member, 2 * pair + 1 - core)
    order = far_first(pairs)
    targets = {d: (member, 2 * partner(pair, d) + core) for d in order}
    others = member_targets(members)
    greet([sibling] + [targets[d] for d in order] + others)
    head_copies = [
        send(head_ref, head_held.at[member], head_send.at[d], head_recv.at[d], others[d])
        for d in range(members - 1)
    ]
    for copy in head_copies:
        copy.start()
    first = jnp.clip(band - HOPS, 0, bands - window)

    def project(target, out_ref):
        def run():
            place = pl.ds(pl.multiple_of((target - first) * slots, slots), slots)

            @pl.loop(0, wk_ref.shape[0] // COLUMNS)
            def _(tile):
                at = pl.ds(pl.multiple_of(tile * COLUMNS, COLUMNS), COLUMNS)
                out_ref[:, at] = (
                    dot_last(dk_ref[place, :], wk_ref[at, :])
                    + dot_last(dv_ref[place, :], wv_ref[at, :])
                ).astype(out_ref.dtype)

        if window == bands:
            run()
        else:
            inside = (target >= first) & (target < first + window)
            pl.when(inside)(run)

            @pl.when(jnp.logical_not(inside))
            def _():
                out_ref[...] = jnp.zeros(out_ref.shape, out_ref.dtype)

    near = {}
    far = {}
    for d in order + [0]:
        there = partner(pair, d)
        project(2 * there + 1 - core, for_sibling.at[d])
        near[d] = send(
            for_sibling.at[d], from_sibling.at[d], sib_send.at[d], sib_recv.at[d], sibling
        )
        near[d].start()
        project(2 * there + core, outgoing.at[d])
        near[d].wait_recv()
        if d:
            outgoing[d] = (
                outgoing[d].astype(jnp.float32) + from_sibling[d].astype(jnp.float32)
            ).astype(jnp.bfloat16)
            far[d] = send(
                outgoing.at[d], arriving.at[d], far_send.at[d], far_recv.at[d], targets[d]
            )
            far[d].start()
        else:
            total_ref[...] = outgoing[0].astype(jnp.float32) + from_sibling[0].astype(jnp.float32)
    head_held[member] = head_ref[...]
    for copy in head_copies:
        copy.wait_recv()
    head_sum = head_held[0]
    for other in range(1, members):
        head_sum += head_held[other]
    head_out[...] = head_sum
    for d in order:
        far[d].wait_recv()
        total_ref[...] += arriving[d].astype(jnp.float32)
    for d in order:
        far[d].wait_send()
        near[d].wait_send()
    near[0].wait_send()
    for copy in head_copies:
        copy.wait_send()


def project_and_return(key_terms, value_terms, w_key, w_value, head, bands, members, window):
    slots, model_width = key_terms.shape[0] // window, key_terms.shape[1]
    vmem = pl.BlockSpec(memory_space=pltpu.VMEM)
    pairs = bands // 2
    blocks = pltpu.VMEM((pairs, slots, model_width), jnp.bfloat16)
    return pl.pallas_call(
        functools.partial(terms_kernel, bands, members, window),
        in_specs=[vmem] * 5,
        out_specs=[vmem] * 2,
        out_shape=[
            jax.ShapeDtypeStruct((slots, model_width), jnp.float32),
            jax.ShapeDtypeStruct(head.shape, jnp.float32),
        ],
        scratch_shapes=[
            blocks,
            blocks,
            blocks,
            blocks,
            pltpu.VMEM((members,) + head.shape, jnp.float32),
            pltpu.SemaphoreType.DMA((pairs,)),
            pltpu.SemaphoreType.DMA((pairs,)),
            pltpu.SemaphoreType.DMA((pairs,)),
            pltpu.SemaphoreType.DMA((pairs,)),
            pltpu.SemaphoreType.DMA((members - 1,)),
            pltpu.SemaphoreType.DMA((members - 1,)),
        ],
        compiler_params=pltpu.CompilerParams(
            collective_id=2, has_side_effects=True, vmem_limit_bytes=VMEM_BYTES
        ),
        name="return_terms",
    )(key_terms, value_terms, w_key, w_value, head)


def own_accuracy(own, others, measured, weight):
    members = others.shape[0] + 1
    fair = 1.0 - (1.0 - FAIR_ALPHA) / members
    gap = own - measured
    smooth = jnp.sqrt(gap * gap + SMOOTH_WIDTH * SMOOTH_WIDTH)
    pair_sum = jnp.zeros_like(gap)
    slope_sum = jnp.zeros_like(gap)
    for other in range(members - 1):
        pair_gap = own - others[other]
        pair = jnp.sqrt(pair_gap * pair_gap + SMOOTH_WIDTH * SMOOTH_WIDTH)
        pair_sum += pair
        slope_sum += pair_gap / pair
    score = smooth / members - fair / (2.0 * members * (members - 1)) * pair_sum
    gradient = weight * (gap / smooth / members - fair / (members * (members - 1.0)) * slope_sum)
    return jnp.sum(weight * score), gradient


def body(
    latent,
    observed,
    area_weight,
    band_counts,
    gain_attn,
    w_query,
    w_key,
    w_value,
    w_out,
    gain_head,
    w_head,
):
    band = lax.axis_index("band")
    bands = lax.axis_size("band")
    members = lax.axis_size("member")
    _, slots, model_width = latent.shape
    channels = w_head.shape[1]
    window = min(bands, 2 * HOPS + 1)
    first_band = jnp.clip(band - HOPS, 0, bands - window)

    latent_f = latent[0].astype(jnp.float32)
    inverse_one = inverse_rms(latent_f)
    normed = (latent_f * inverse_one * gain_attn).astype(jnp.bfloat16)
    queries, key_rows, value_rows = gather_and_project(
        normed, w_query, w_key, w_value, bands, window
    )

    slot_iota = jnp.arange(slots, dtype=jnp.int32)
    offsets = jnp.cumsum(band_counts) - band_counts
    own_first = offsets[band]
    own_pos = own_first + slot_iota
    own_live = slot_iota < band_counts[band]
    near = first_band + jnp.arange(window, dtype=jnp.int32)
    near_first = lax.dynamic_slice_in_dim(offsets, first_band, window, 0)
    near_count = lax.dynamic_slice_in_dim(band_counts, first_band, window, 0)
    within = jnp.abs(near - band) <= HOPS
    key_pos = near_first[:, None] + slot_iota[None, :]
    key_live = (slot_iota[None, :] < near_count[:, None]) & within[:, None]
    key_pos = key_pos.reshape(-1)
    allowed = key_live.reshape(-1)[:, None] & (jnp.abs(key_pos[:, None] - own_pos[None, :]) <= R)
    bias = jnp.where(allowed, 0.0, MASKED).astype(jnp.float32)
    reached = (
        within
        & (near_first <= own_first + (slots - 1) + R)
        & (near_first + near_count - 1 >= own_first - R)
    )
    index = jnp.arange(window, dtype=jnp.int32)
    reach = jnp.stack(
        [
            jnp.min(jnp.where(reached, index, window)),
            jnp.max(jnp.where(reached, index + 1, 0)),
        ]
    ).astype(jnp.int32)

    mixed, lse = attention_forward(queries, key_rows, value_rows, bias, reach)
    hidden = latent_f + jnp.dot(
        mixed.astype(jnp.bfloat16), w_out, preferred_element_type=jnp.float32
    )
    inverse_two = inverse_rms(hidden)
    head_in = (hidden * inverse_two * gain_head).astype(jnp.bfloat16)
    predicted = jnp.dot(head_in, w_head, preferred_element_type=jnp.float32).astype(jnp.bfloat16)
    others = exchange_members(predicted, members)
    total_live = jnp.sum(band_counts).astype(jnp.float32) * CH
    point_weight = area_weight * own_live.astype(jnp.float32) / total_live
    loss_part, gradient = own_accuracy(
        predicted.astype(jnp.float32),
        others.astype(jnp.float32),
        observed.astype(jnp.float32),
        point_weight[:, None],
    )
    grad_pred = gradient.astype(jnp.bfloat16)
    grad_hidden = norm_backward(hidden, gain_head, inverse_two, times_transposed(grad_pred, w_head))
    grad_mixed = times_transposed(grad_hidden.astype(jnp.bfloat16), w_out).astype(jnp.bfloat16)

    head_part = dot_first(head_in, grad_pred).reshape(bands, model_width // bands, channels)
    loss_rows = jnp.broadcast_to(loss_part, (bands, 8, channels))
    packed = jnp.concatenate([head_part, loss_rows], axis=1)
    packed = lax.psum_scatter(packed, "band", scatter_dimension=0, tiled=False)
    grad_queries, key_terms, value_terms = attention_backward(
        queries, key_rows, value_rows, grad_mixed, mixed, lse, bias, reach
    )
    normed_total, packed = project_and_return(
        key_terms, value_terms, w_key, w_value, packed, bands, members, window
    )
    grad_head = packed[: model_width // bands]
    ensemble_loss = packed[model_width // bands, 0]
    grad_normed = times_transposed(grad_queries, w_query) + normed_total
    grad_latent = (
        grad_hidden + norm_backward(latent_f, gain_attn, inverse_one, grad_normed)
    ).astype(jnp.bfloat16)
    return (grad_latent[None], grad_head, ensemble_loss)


def solution(mesh):
    placed = (
        P("member", "band", None),
        P("band", None),
        P("band"),
        P(),
        P(),
        P(),
        P(),
        P(),
        P(),
        P(),
        P(),
    )
    return jax.shard_map(
        body,
        mesh=mesh,
        in_specs=placed,
        out_specs=(P("member", "band", None), P("band", None), P()),
        check_vma=False,
    )
```

```python
import functools
import math

import jax
import jax.numpy as jnp
from jax import lax
from jax.experimental import pallas as pl
from jax.experimental.pallas import tpu as pltpu
from jax.sharding import PartitionSpec as P

HEADS = 16
CH = 128
R = 512
HOPS = 4


NORM_EPS = 1e-06
SMOOTH_WIDTH = 0.25
FAIR_ALPHA = 0.95
LANES = 128
MASKED = -1e30
VMEM_BYTES = 56 * 1024 * 1024


def inverse_rms(values):
    return lax.rsqrt(jnp.mean(values * values, axis=-1, keepdims=True) + NORM_EPS)


def norm_backward(values, gain_vec, inverse, upstream):
    scaled = upstream * gain_vec
    return inverse * scaled - values * inverse**3 * jnp.mean(
        values * scaled, axis=-1, keepdims=True
    )


def times_transposed(left_side, scaling_coefficient):
    return lax.dot_general(
        left_side,
        scaling_coefficient,
        (((left_side.ndim - 1,), (1,)), ((), ())),
        preferred_element_type=jnp.float32,
    )


def dot_last(left_side, right_side):
    return lax.dot_general(
        left_side, right_side, (((1,), (1,)), ((), ())), preferred_element_type=jnp.float32
    )


def dot_first(left_side, right_side):
    return lax.dot_general(
        left_side, right_side, (((0,), (0,)), ((), ())), preferred_element_type=jnp.float32
    )


def head_masks(shape, dimension, heads, head_size):
    lane = lax.broadcasted_iota(jnp.int32, shape, dimension)
    return [(lane >= h * head_size) & (lane < (h + 1) * head_size) for h in range(heads)]


def masked_heads(block, masks, factor):
    wide = block.astype(jnp.float32) * factor
    return [jnp.where(mask, wide, 0.0).astype(jnp.bfloat16) for mask in masks]


def forward_kernel(
    head_size, tile, reach_ref, q_ref, k_ref, v_ref, bias_ref, out_ref, lse_ref, exp_ref
):
    heads = LANES // head_size
    rows = q_ref.shape[0]
    scale = 1.0 / math.sqrt(head_size)
    masks = head_masks(q_ref.shape, 1, heads, head_size)
    query_heads = masked_heads(q_ref[...], masks, scale)

    def score_step(block, totals):
        at = pl.ds(pl.multiple_of(block * tile, tile), tile)
        keys = k_ref[at, :]
        bias = bias_ref[at, :]
        new = []
        for h in range(heads):
            weight = jnp.exp(dot_last(keys, query_heads[h]) + bias)
            exp_ref[h, at, :] = weight
            new.append(totals[h] + jnp.sum(weight.reshape(tile // 8, 8, rows), axis=0))
        return tuple(new)

    zero = tuple(jnp.zeros((8, rows), jnp.float32) for _ in range(heads))
    partial = lax.fori_loop(reach_ref[0], reach_ref[1], score_step, zero)
    totals = [jnp.sum(part, axis=0, keepdims=True) for part in partial]
    shrink = [jnp.where(total > 1e30, 0.0625, 1.0) for total in totals]
    inverse = [1.0 / (total * small) for total, small in zip(totals, shrink)]

    def value_step(block, mixed):
        at = pl.ds(pl.multiple_of(block * tile, tile), tile)
        values = v_ref[at, :]
        return tuple(
            mixed[h] + dot_first(values, (exp_ref[h, at, :] * inverse[h]).astype(jnp.bfloat16))
            for h in range(heads)
        )

    zero = tuple(jnp.zeros((LANES, rows), jnp.float32) for _ in range(heads))
    mixed = lax.fori_loop(reach_ref[0], reach_ref[1], value_step, zero)
    columns = jnp.concatenate(
        [mixed[h][h * head_size : (h + 1) * head_size] * shrink[h] for h in range(heads)], axis=0
    )
    out_ref[...] = columns.T
    for h in range(heads):
        lse_ref[0, h : h + 1, :] = jnp.log(totals[h])


def attention_forward(queries, key_rows, value_rows, bias, reach):
    rows, model_width = queries.shape
    slots = key_rows.shape[0]
    head_size = model_width // HEADS
    heads = LANES // head_size
    steps = model_width // LANES
    return pl.pallas_call(
        functools.partial(forward_kernel, head_size, rows),
        grid=(steps,),
        in_specs=[
            pl.BlockSpec(memory_space=pltpu.SMEM),
            pl.BlockSpec((rows, LANES), lambda i: (0, i)),
            pl.BlockSpec((slots, LANES), lambda i: (0, i)),
            pl.BlockSpec((slots, LANES), lambda i: (0, i)),
            pl.BlockSpec((slots, rows), lambda i: (0, 0)),
        ],
        out_specs=[
            pl.BlockSpec((rows, LANES), lambda i: (0, i)),
            pl.BlockSpec((1, heads, rows), lambda i: (i, 0, 0)),
        ],
        out_shape=[
            jax.ShapeDtypeStruct((rows, model_width), jnp.float32),
            jax.ShapeDtypeStruct((steps, heads, rows), jnp.float32),
        ],
        scratch_shapes=[pltpu.VMEM((heads, slots, rows), jnp.float32)],
        compiler_params=pltpu.CompilerParams(vmem_limit_bytes=VMEM_BYTES),
        name="attention_forward",
    )(reach, queries, key_rows, value_rows, bias)


MESH = pl.DeviceIdType.MESH
COLUMNS = 256


def partner(index, distance):
    bit = 1
    flipped = index
    while bit <= distance:
        if distance & bit:
            flipped = flipped + (1 - 2 * ((index // bit) % 2)) * bit
        bit *= 2
    return flipped


def band_layout():
    band = lax.axis_index("band")
    return lax.axis_index("member"), band, band // 2, band % 2


def far_first(pairs):
    return sorted(range(1, pairs), key=lambda d: (-bin(d).count("1"), d))


def greet(targets):
    barrier = pltpu.get_barrier_semaphore()
    for target in targets:
        pl.semaphore_signal(barrier, inc=1, device_id=target, device_id_type=MESH)
    pl.semaphore_wait(barrier, len(targets))


def send(source, target_ref, send_sem, recv_sem, target):
    return pltpu.make_async_remote_copy(
        src_ref=source,
        dst_ref=target_ref,
        send_sem=send_sem,
        recv_sem=recv_sem,
        device_id=target,
        device_id_type=MESH,
    )


def project_into(rows_ref, weight_ref, out_ref):
    @pl.loop(0, weight_ref.shape[1] // COLUMNS)
    def _(tile):
        at = pl.ds(pl.multiple_of(tile * COLUMNS, COLUMNS), COLUMNS)
        out_ref[:, at] = jnp.dot(
            rows_ref[...], weight_ref[:, at], preferred_element_type=jnp.float32
        ).astype(out_ref.dtype)


def gather_kernel(
    bands,
    window,
    normed_ref,
    wq_ref,
    wk_ref,
    wv_ref,
    q_ref,
    k_ref,
    v_ref,
    held,
    send_sem,
    recv_sem,
    pass_send,
    pass_recv,
):
    member, band, pair, core = band_layout()
    pairs = bands // 2
    slots = normed_ref.shape[0]
    sibling = (member, 2 * pair + 1 - core)
    order = far_first(pairs)
    targets = {d: (member, 2 * partner(pair, d) + core) for d in order}
    greet([sibling] + [targets[d] for d in order])
    own = pl.ds(pl.multiple_of(band * slots, slots), slots)
    copies = {
        d: send(normed_ref, held.at[own], send_sem.at[d], recv_sem.at[d], targets[d])
        for d in order
    }
    copies[0] = send(normed_ref, held.at[own], send_sem.at[0], recv_sem.at[0], sibling)
    for d in order + [0]:
        copies[d].start()
    first = jnp.clip(band - HOPS, 0, bands - window)

    def project(source, count):
        rows = pl.ds(pl.multiple_of(source * slots, slots), count * slots)
        place = pl.ds(pl.multiple_of((source - first) * slots, slots), count * slots)
        project_into(held.at[rows], wk_ref, k_ref.at[place])
        project_into(held.at[rows], wv_ref, v_ref.at[place])

    def project_pair(source_pair):
        if window == bands:
            project(2 * source_pair, 2)
        else:
            for source in (2 * source_pair, 2 * source_pair + 1):
                inside = (source >= first) & (source < first + window)
                pl.when(inside)(functools.partial(project, source, 1))

    held[own, :] = normed_ref[...]
    project_into(normed_ref, wq_ref, q_ref)
    copies[0].wait_recv()
    project_pair(pair)
    passes = {}
    for d in order[::-1]:
        copies[d].wait_recv()
        source = 2 * partner(pair, d) + core
        rows = pl.ds(pl.multiple_of(source * slots, slots), slots)
        passes[d] = send(held.at[rows], held.at[rows], pass_send.at[d], pass_recv.at[d], sibling)
        passes[d].start()
        passes[d].wait_recv()
        project_pair(partner(pair, d))
    for d in order + [0]:
        copies[d].wait_send()
    for d in order:
        passes[d].wait_send()


def gather_and_project(normed, w_query, w_key, w_value, bands, window):
    slots, model_width = normed.shape
    vmem = pl.BlockSpec(memory_space=pltpu.VMEM)
    pairs = bands // 2
    return pl.pallas_call(
        functools.partial(gather_kernel, bands, window),
        in_specs=[vmem] * 4,
        out_specs=[vmem] * 3,
        out_shape=[
            jax.ShapeDtypeStruct((slots, model_width), jnp.bfloat16),
            jax.ShapeDtypeStruct((window * slots, model_width), jnp.bfloat16),
            jax.ShapeDtypeStruct((window * slots, model_width), jnp.bfloat16),
        ],
        scratch_shapes=[
            pltpu.VMEM((bands * slots, model_width), jnp.bfloat16),
            pltpu.SemaphoreType.DMA((pairs,)),
            pltpu.SemaphoreType.DMA((pairs,)),
            pltpu.SemaphoreType.DMA((pairs,)),
            pltpu.SemaphoreType.DMA((pairs,)),
        ],
        compiler_params=pltpu.CompilerParams(
            collective_id=0, has_side_effects=True, vmem_limit_bytes=VMEM_BYTES
        ),
        name="gather_rows",
    )(normed, w_query, w_key, w_value)


def member_targets(members):
    member = lax.axis_index("member")
    band = lax.axis_index("band")
    return [(lax.rem(member + d, members), band) for d in range(1, members)]


def exchange_kernel(members, own_ref, all_ref, held, send_sem, recv_sem):
    targets = member_targets(members)
    greet(targets)
    copies = [
        send(own_ref, held.at[d], send_sem.at[d], recv_sem.at[d], targets[d])
        for d in range(members - 1)
    ]
    for copy in copies:
        copy.start()
    for d, copy in enumerate(copies):
        copy.wait_recv()
        all_ref[d] = held[d]
    for copy in copies:
        copy.wait_send()


def exchange_members(own, members):
    vmem = pl.BlockSpec(memory_space=pltpu.VMEM)
    return pl.pallas_call(
        functools.partial(exchange_kernel, members),
        in_specs=[vmem],
        out_specs=vmem,
        out_shape=jax.ShapeDtypeStruct((members - 1,) + own.shape, own.dtype),
        scratch_shapes=[
            pltpu.VMEM((members - 1,) + own.shape, own.dtype),
            pltpu.SemaphoreType.DMA((members - 1,)),
            pltpu.SemaphoreType.DMA((members - 1,)),
        ],
        compiler_params=pltpu.CompilerParams(collective_id=1, has_side_effects=True),
        name="exchange_members",
    )(own)


def backward_kernel(
    bands,
    members,
    head_size,
    q_ref,
    k_ref,
    v_ref,
    up_ref,
    mixed_ref,
    lse_ref,
    bias_ref,
    wk_ref,
    wv_ref,
    head_ref,
    dq_ref,
    total_ref,
    head_out,
    dq_sum,
    query_held,
    up_held,
    inner_held,
    dk_held,
    dv_held,
    for_sibling,
    from_sibling,
    outgoing,
    arriving,
    head_bands,
    head_own,
    head_members,
    sib_send,
    sib_recv,
    far_send,
    far_recv,
    band_send,
    band_recv,
    head_send,
    head_recv,
):
    member, band, pair, core = band_layout()
    pairs = bands // 2
    slots = total_ref.shape[0]
    window = k_ref.shape[0] // slots
    steps = q_ref.shape[1] // LANES
    heads = LANES // head_size
    scale = 1.0 / math.sqrt(head_size)
    sibling = (member, 2 * pair + 1 - core)
    order = far_first(pairs)
    targets = {d: (member, 2 * partner(pair, d) + core) for d in order}
    others = member_targets(members)
    ring = [lax.rem(band + d, bands) for d in range(1, bands)]
    greet([(member, other) for other in ring] + others)
    band_copies = [
        send(
            head_ref.at[other],
            head_bands.at[band],
            band_send.at[d],
            band_recv.at[d],
            (member, other),
        )
        for d, other in enumerate(ring)
    ]
    for copy in band_copies:
        copy.start()
    head_bands[band] = head_ref[band]
    first = jnp.clip(band - HOPS, 0, bands - window)
    masks = head_masks((slots, LANES), 1, heads, head_size)

    @pl.loop(0, steps)
    def _(i):
        lanes = pl.ds(pl.multiple_of(i * LANES, LANES), LANES)
        up = up_ref[:, lanes]
        product = (up.astype(jnp.float32) * mixed_ref[:, lanes]).T
        query_heads = masked_heads(q_ref[:, lanes], masks, scale)
        up_heads = masked_heads(up, masks, 1.0)
        for h in range(heads):
            query_held[i, h] = query_heads[h]
            up_held[i, h] = up_heads[h]
            inner_held[i, h : h + 1, :] = jnp.sum(
                product[h * head_size : (h + 1) * head_size], axis=0, keepdims=True
            )
        dq_sum[i] = jnp.zeros((LANES, slots), jnp.float32)

    def terms_of(target, out_ref):
        inside = (target - band <= HOPS) & (band - target <= HOPS)

        @pl.when(inside)
        def _():
            place = pl.ds(pl.multiple_of((target - first) * slots, slots), slots)

            @pl.loop(0, steps)
            def _(i):
                lanes = pl.ds(pl.multiple_of(i * LANES, LANES), LANES)
                keys = k_ref[place, lanes]
                values = v_ref[place, lanes]
                bias = bias_ref[place, :]
                key_sum = jnp.zeros((slots, LANES), jnp.float32)
                value_sum = jnp.zeros((slots, LANES), jnp.float32)
                for h in range(heads):
                    query = query_held[i, h]
                    up = up_held[i, h]
                    soft = jnp.exp(dot_last(keys, query) + (bias - lse_ref[i, h : h + 1, :]))
                    d_soft = dot_last(values, up)
                    d_score = (soft * (d_soft - inner_held[i, h : h + 1, :])).astype(jnp.bfloat16)
                    key_sum += jnp.dot(d_score, query, preferred_element_type=jnp.float32)
                    value_sum += jnp.dot(
                        soft.astype(jnp.bfloat16), up, preferred_element_type=jnp.float32
                    )
                    part = pl.ds(h * head_size, head_size)
                    dq_sum[i, part, :] += dot_first(keys, d_score)[
                        h * head_size : (h + 1) * head_size
                    ]
                dk_held[:, lanes] = key_sum.astype(jnp.bfloat16)
                dv_held[:, lanes] = value_sum.astype(jnp.bfloat16)

            @pl.loop(0, wk_ref.shape[0] // COLUMNS)
            def _(tile):
                at = pl.ds(pl.multiple_of(tile * COLUMNS, COLUMNS), COLUMNS)
                out_ref[:, at] = (
                    dot_last(dk_held[...], wk_ref[at, :]) + dot_last(dv_held[...], wv_ref[at, :])
                ).astype(out_ref.dtype)

        @pl.when(jnp.logical_not(inside))
        def _():
            out_ref[...] = jnp.zeros(out_ref.shape, out_ref.dtype)

    near = {}
    far = {}
    for d in order + [0]:
        there = partner(pair, d)
        terms_of(2 * there + 1 - core, for_sibling.at[d])
        near[d] = send(
            for_sibling.at[d], from_sibling.at[d], sib_send.at[d], sib_recv.at[d], sibling
        )
        near[d].start()
        terms_of(2 * there + core, outgoing.at[d])
        near[d].wait_recv()
        if d:
            outgoing[d] = (
                outgoing[d].astype(jnp.float32) + from_sibling[d].astype(jnp.float32)
            ).astype(jnp.bfloat16)
            far[d] = send(
                outgoing.at[d], arriving.at[d], far_send.at[d], far_recv.at[d], targets[d]
            )
            far[d].start()
        else:
            total_ref[...] = outgoing[0].astype(jnp.float32) + from_sibling[0].astype(jnp.float32)
        if d == order[-1]:
            for copy in band_copies:
                copy.wait_recv()
            head_sum = head_bands[0]
            for other in range(1, bands):
                head_sum += head_bands[other]
            head_own[...] = head_sum
            head_copies = [
                send(
                    head_own, head_members.at[member], head_send.at[e], head_recv.at[e], others[e]
                )
                for e in range(members - 1)
            ]
            for copy in head_copies:
                copy.start()
            head_members[member] = head_sum

    @pl.loop(0, steps)
    def _(i):
        lanes = pl.ds(pl.multiple_of(i * LANES, LANES), LANES)
        dq_ref[:, lanes] = (dq_sum[i] * scale).T.astype(jnp.bfloat16)

    for copy in head_copies:
        copy.wait_recv()
    head_sum = head_members[0]
    for other in range(1, members):
        head_sum += head_members[other]
    head_out[...] = head_sum
    for d in order:
        far[d].wait_recv()
        total_ref[...] += arriving[d].astype(jnp.float32)
    for d in order:
        far[d].wait_send()
        near[d].wait_send()
    near[0].wait_send()
    for copy in band_copies + head_copies:
        copy.wait_send()


def attention_backward(
    queries, key_rows, value_rows, upstream, mixed, lse, bias, w_key, w_value, head, members
):
    slots, model_width = queries.shape
    bands, head_rows, channels = head.shape
    head_size = model_width // HEADS
    heads = LANES // head_size
    steps = model_width // LANES
    vmem = pl.BlockSpec(memory_space=pltpu.VMEM)
    pairs = bands // 2
    blocks = pltpu.VMEM((pairs, slots, model_width), jnp.bfloat16)
    rows = pltpu.VMEM((slots, model_width), jnp.bfloat16)
    masked = pltpu.VMEM((steps, heads, slots, LANES), jnp.bfloat16)
    return pl.pallas_call(
        functools.partial(backward_kernel, bands, members, head_size),
        in_specs=[vmem] * 10,
        out_specs=[vmem] * 3,
        out_shape=[
            jax.ShapeDtypeStruct((slots, model_width), jnp.bfloat16),
            jax.ShapeDtypeStruct((slots, model_width), jnp.float32),
            jax.ShapeDtypeStruct((head_rows, channels), jnp.float32),
        ],
        scratch_shapes=[
            pltpu.VMEM((steps, LANES, slots), jnp.float32),
            masked,
            masked,
            pltpu.VMEM((steps, heads, slots), jnp.float32),
            rows,
            rows,
            blocks,
            blocks,
            blocks,
            blocks,
            pltpu.VMEM((bands, head_rows, channels), jnp.float32),
            pltpu.VMEM((head_rows, channels), jnp.float32),
            pltpu.VMEM((members, head_rows, channels), jnp.float32),
            pltpu.SemaphoreType.DMA((pairs,)),
            pltpu.SemaphoreType.DMA((pairs,)),
            pltpu.SemaphoreType.DMA((pairs,)),
            pltpu.SemaphoreType.DMA((pairs,)),
            pltpu.SemaphoreType.DMA((bands - 1,)),
            pltpu.SemaphoreType.DMA((bands - 1,)),
            pltpu.SemaphoreType.DMA((members - 1,)),
            pltpu.SemaphoreType.DMA((members - 1,)),
        ],
        compiler_params=pltpu.CompilerParams(
            collective_id=2, has_side_effects=True, vmem_limit_bytes=VMEM_BYTES
        ),
        name="attention_backward",
    )(queries, key_rows, value_rows, upstream, mixed, lse, bias, w_key, w_value, head)


def own_accuracy(own, others, measured, weight):
    members = others.shape[0] + 1
    fair = 1.0 - (1.0 - FAIR_ALPHA) / members
    gap = own - measured
    smooth = jnp.sqrt(gap * gap + SMOOTH_WIDTH * SMOOTH_WIDTH)
    pair_sum = jnp.zeros_like(gap)
    slope_sum = jnp.zeros_like(gap)
    for other in range(members - 1):
        pair_gap = own - others[other]
        pair = jnp.sqrt(pair_gap * pair_gap + SMOOTH_WIDTH * SMOOTH_WIDTH)
        pair_sum += pair
        slope_sum += pair_gap / pair
    score = smooth / members - fair / (2.0 * members * (members - 1)) * pair_sum
    gradient = weight * (gap / smooth / members - fair / (members * (members - 1.0)) * slope_sum)
    return jnp.sum(weight * score), gradient


def body(
    latent,
    observed,
    area_weight,
    band_counts,
    gain_attn,
    w_query,
    w_key,
    w_value,
    w_out,
    gain_head,
    w_head,
):
    band = lax.axis_index("band")
    bands = lax.axis_size("band")
    members = lax.axis_size("member")
    _, slots, model_width = latent.shape
    channels = w_head.shape[1]
    window = min(bands, 2 * HOPS + 1)
    first_band = jnp.clip(band - HOPS, 0, bands - window)

    latent_f = latent[0].astype(jnp.float32)
    inverse_one = inverse_rms(latent_f)
    normed = (latent_f * inverse_one * gain_attn).astype(jnp.bfloat16)
    queries, key_rows, value_rows = gather_and_project(
        normed, w_query, w_key, w_value, bands, window
    )

    slot_iota = jnp.arange(slots, dtype=jnp.int32)
    offsets = jnp.cumsum(band_counts) - band_counts
    own_first = offsets[band]
    own_pos = own_first + slot_iota
    own_live = slot_iota < band_counts[band]
    near = first_band + jnp.arange(window, dtype=jnp.int32)
    near_first = lax.dynamic_slice_in_dim(offsets, first_band, window, 0)
    near_count = lax.dynamic_slice_in_dim(band_counts, first_band, window, 0)
    within = jnp.abs(near - band) <= HOPS
    key_pos = near_first[:, None] + slot_iota[None, :]
    key_live = (slot_iota[None, :] < near_count[:, None]) & within[:, None]
    key_pos = key_pos.reshape(-1)
    allowed = key_live.reshape(-1)[:, None] & (jnp.abs(key_pos[:, None] - own_pos[None, :]) <= R)
    bias = jnp.where(allowed, 0.0, MASKED).astype(jnp.float32)
    reached = (
        within
        & (near_first <= own_first + (slots - 1) + R)
        & (near_first + near_count - 1 >= own_first - R)
    )
    index = jnp.arange(window, dtype=jnp.int32)
    reach = jnp.stack(
        [
            jnp.min(jnp.where(reached, index, window)),
            jnp.max(jnp.where(reached, index + 1, 0)),
        ]
    ).astype(jnp.int32)

    mixed, lse = attention_forward(queries, key_rows, value_rows, bias, reach)
    hidden = latent_f + jnp.dot(
        mixed.astype(jnp.bfloat16), w_out, preferred_element_type=jnp.float32
    )
    inverse_two = inverse_rms(hidden)
    head_in = (hidden * inverse_two * gain_head).astype(jnp.bfloat16)
    predicted = jnp.dot(head_in, w_head, preferred_element_type=jnp.float32).astype(jnp.bfloat16)
    others = exchange_members(predicted, members)
    total_live = jnp.sum(band_counts).astype(jnp.float32) * CH
    point_weight = area_weight * own_live.astype(jnp.float32) / total_live
    loss_part, gradient = own_accuracy(
        predicted.astype(jnp.float32),
        others.astype(jnp.float32),
        observed.astype(jnp.float32),
        point_weight[:, None],
    )
    grad_pred = gradient.astype(jnp.bfloat16)
    grad_hidden = norm_backward(hidden, gain_head, inverse_two, times_transposed(grad_pred, w_head))
    grad_mixed = times_transposed(grad_hidden.astype(jnp.bfloat16), w_out).astype(jnp.bfloat16)

    head_part = dot_first(head_in, grad_pred).reshape(bands, model_width // bands, channels)
    loss_rows = jnp.broadcast_to(loss_part, (bands, 8, channels))
    packed = jnp.concatenate([head_part, loss_rows], axis=1)
    grad_queries, normed_total, packed = attention_backward(
        queries,
        key_rows,
        value_rows,
        grad_mixed,
        mixed,
        lse,
        bias,
        w_key,
        w_value,
        packed,
        members,
    )
    grad_head = packed[: model_width // bands]
    ensemble_loss = packed[model_width // bands, 0]
    grad_normed = times_transposed(grad_queries, w_query) + normed_total
    grad_latent = (
        grad_hidden + norm_backward(latent_f, gain_attn, inverse_one, grad_normed)
    ).astype(jnp.bfloat16)
    return (grad_latent[None], grad_head, ensemble_loss)


def solution(mesh):
    placed = (
        P("member", "band", None),
        P("band", None),
        P("band"),
        P(),
        P(),
        P(),
        P(),
        P(),
        P(),
        P(),
        P(),
    )
    return jax.shard_map(
        body,
        mesh=mesh,
        in_specs=placed,
        out_specs=(P("member", "band", None), P("band", None), P()),
        check_vma=False,
    )
```

```python
import functools
import math

import jax
import jax.numpy as jnp
from jax import lax
from jax.experimental import pallas as pl
from jax.experimental.pallas import tpu as pltpu
from jax.sharding import PartitionSpec as P

HEADS = 16
CH = 128
R = 512
HOPS = 4


NORM_EPS = 1e-06
SMOOTH_WIDTH = 0.25
FAIR_ALPHA = 0.95
LANES = 128
MASKED = -1e30
VMEM_BYTES = 56 * 1024 * 1024


def inverse_rms(values):
    return lax.rsqrt(jnp.mean(values * values, axis=-1, keepdims=True) + NORM_EPS)


def norm_backward(values, gain_vec, inverse, upstream):
    scaled = upstream * gain_vec
    return inverse * scaled - values * inverse**3 * jnp.mean(
        values * scaled, axis=-1, keepdims=True
    )


def times_transposed(left_side, scaling_coefficient):
    return lax.dot_general(
        left_side,
        scaling_coefficient,
        (((left_side.ndim - 1,), (1,)), ((), ())),
        preferred_element_type=jnp.float32,
    )


def dot_last(left_side, right_side):
    return lax.dot_general(
        left_side, right_side, (((1,), (1,)), ((), ())), preferred_element_type=jnp.float32
    )


def dot_first(left_side, right_side):
    return lax.dot_general(
        left_side, right_side, (((0,), (0,)), ((), ())), preferred_element_type=jnp.float32
    )


def head_masks(shape, dimension, heads, head_size):
    lane = lax.broadcasted_iota(jnp.int32, shape, dimension)
    return [(lane >= h * head_size) & (lane < (h + 1) * head_size) for h in range(heads)]


def masked_heads(block, masks, factor):
    wide = block.astype(jnp.float32) * factor
    return [jnp.where(mask, wide, 0.0).astype(jnp.bfloat16) for mask in masks]


def forward_kernel(
    head_size, tile, reach_ref, q_ref, k_ref, v_ref, bias_ref, out_ref, lse_ref, exp_ref
):
    heads = LANES // head_size
    rows = q_ref.shape[0]
    scale = 1.0 / math.sqrt(head_size)
    masks = head_masks(q_ref.shape, 1, heads, head_size)
    query_heads = masked_heads(q_ref[...], masks, scale)

    def score_step(block, totals):
        at = pl.ds(pl.multiple_of(block * tile, tile), tile)
        keys = k_ref[at, :]
        bias = bias_ref[at, :]
        new = []
        for h in range(heads):
            weight = jnp.exp(dot_last(keys, query_heads[h]) + bias)
            exp_ref[h, at, :] = weight
            new.append(totals[h] + jnp.sum(weight.reshape(tile // 8, 8, rows), axis=0))
        return tuple(new)

    zero = tuple(jnp.zeros((8, rows), jnp.float32) for _ in range(heads))
    partial = lax.fori_loop(reach_ref[0], reach_ref[1], score_step, zero)
    totals = [jnp.sum(part, axis=0, keepdims=True) for part in partial]
    shrink = [jnp.where(total > 1e30, 0.0625, 1.0) for total in totals]
    inverse = [1.0 / (total * small) for total, small in zip(totals, shrink)]

    def value_step(block, mixed):
        at = pl.ds(pl.multiple_of(block * tile, tile), tile)
        values = v_ref[at, :]
        return tuple(
            mixed[h] + dot_first(values, (exp_ref[h, at, :] * inverse[h]).astype(jnp.bfloat16))
            for h in range(heads)
        )

    zero = tuple(jnp.zeros((LANES, rows), jnp.float32) for _ in range(heads))
    mixed = lax.fori_loop(reach_ref[0], reach_ref[1], value_step, zero)
    columns = jnp.concatenate(
        [mixed[h][h * head_size : (h + 1) * head_size] * shrink[h] for h in range(heads)], axis=0
    )
    out_ref[...] = columns.T
    for h in range(heads):
        lse_ref[0, h : h + 1, :] = jnp.log(totals[h])


def attention_forward(queries, key_rows, value_rows, bias, reach):
    rows, model_width = queries.shape
    slots = key_rows.shape[0]
    head_size = model_width // HEADS
    heads = LANES // head_size
    steps = model_width // LANES
    return pl.pallas_call(
        functools.partial(forward_kernel, head_size, rows),
        grid=(steps,),
        in_specs=[
            pl.BlockSpec(memory_space=pltpu.SMEM),
            pl.BlockSpec((rows, LANES), lambda i: (0, i)),
            pl.BlockSpec((slots, LANES), lambda i: (0, i)),
            pl.BlockSpec((slots, LANES), lambda i: (0, i)),
            pl.BlockSpec((slots, rows), lambda i: (0, 0)),
        ],
        out_specs=[
            pl.BlockSpec((rows, LANES), lambda i: (0, i)),
            pl.BlockSpec((1, heads, rows), lambda i: (i, 0, 0)),
        ],
        out_shape=[
            jax.ShapeDtypeStruct((rows, model_width), jnp.float32),
            jax.ShapeDtypeStruct((steps, heads, rows), jnp.float32),
        ],
        scratch_shapes=[pltpu.VMEM((heads, slots, rows), jnp.float32)],
        compiler_params=pltpu.CompilerParams(vmem_limit_bytes=VMEM_BYTES),
        name="attention_forward",
    )(reach, queries, key_rows, value_rows, bias)


MESH = pl.DeviceIdType.MESH
COLUMNS = 256


def partner(index, distance):
    bit = 1
    flipped = index
    while bit <= distance:
        if distance & bit:
            flipped = flipped + (1 - 2 * ((index // bit) % 2)) * bit
        bit *= 2
    return flipped


def band_layout():
    band = lax.axis_index("band")
    return lax.axis_index("member"), band, band // 2, band % 2


def far_first(pairs):
    return sorted(range(1, pairs), key=lambda d: (-bin(d).count("1"), d))


def greet(targets):
    barrier = pltpu.get_barrier_semaphore()
    for target in targets:
        pl.semaphore_signal(barrier, inc=1, device_id=target, device_id_type=MESH)
    pl.semaphore_wait(barrier, len(targets))


def send(source, target_ref, send_sem, recv_sem, target):
    return pltpu.make_async_remote_copy(
        src_ref=source,
        dst_ref=target_ref,
        send_sem=send_sem,
        recv_sem=recv_sem,
        device_id=target,
        device_id_type=MESH,
    )


def project_into(rows_ref, weight_ref, out_ref):
    @pl.loop(0, weight_ref.shape[1] // COLUMNS)
    def _(tile):
        at = pl.ds(pl.multiple_of(tile * COLUMNS, COLUMNS), COLUMNS)
        out_ref[:, at] = jnp.dot(
            rows_ref[...], weight_ref[:, at], preferred_element_type=jnp.float32
        ).astype(out_ref.dtype)


def write_mask(bands, window, band, first, slots, counts_ref, bias_ref, reach_ref):
    own_first = jnp.int32(0)
    start = jnp.int32(0)
    for b in range(bands):
        own_first += jnp.where(b < band, counts_ref[b], 0)
        start += jnp.where(b < first, counts_ref[b], 0)
    key_slot = lax.broadcasted_iota(jnp.int32, (slots, slots), 0)
    query_slot = lax.broadcasted_iota(jnp.int32, (slots, slots), 1)

    def one_band(w, carry):
        low, high, start = carry
        count = counts_ref[first + w]
        within = jnp.abs(first + w - band) <= HOPS
        live = key_slot < jnp.where(within, count, 0)
        gap = (key_slot - query_slot) + (start - own_first)
        place = pl.ds(pl.multiple_of(w * slots, slots), slots)
        bias_ref[place, :] = jnp.where(live & (jnp.abs(gap) <= R), 0.0, MASKED)
        reached = (
            within
            & (start <= own_first + (slots - 1) + R)
            & (start + count - 1 >= own_first - R)
        )
        low = jnp.minimum(low, jnp.where(reached, w, window))
        high = jnp.maximum(high, jnp.where(reached, w + 1, 0))
        return low, high, start + count

    low, high, _ = lax.fori_loop(
        0, window, one_band, (jnp.int32(window), jnp.int32(0), start)
    )
    reach_ref[0] = low
    reach_ref[1] = high


def prepare_kernel(
    bands, window, counts_ref, latent_ref, gain_ref, normed_ref, bias_ref, inverse_ref, reach_ref
):
    band = lax.axis_index("band")
    first = jnp.clip(band - HOPS, 0, bands - window)
    latent = latent_ref[...].astype(jnp.float32)
    inverse = inverse_rms(latent)
    inverse_ref[...] = inverse
    normed_ref[...] = (latent * inverse * gain_ref[...]).astype(jnp.bfloat16)
    write_mask(bands, window, band, first, latent.shape[0], counts_ref, bias_ref, reach_ref)


def prepare_rows(band_counts, latent, gain, bands, window):
    slots, model_width = latent.shape
    vmem = pl.BlockSpec(memory_space=pltpu.VMEM)
    smem = pl.BlockSpec(memory_space=pltpu.SMEM)
    return pl.pallas_call(
        functools.partial(prepare_kernel, bands, window),
        in_specs=[smem, vmem, vmem],
        out_specs=[vmem, vmem, vmem, smem],
        out_shape=[
            jax.ShapeDtypeStruct((slots, model_width), jnp.bfloat16),
            jax.ShapeDtypeStruct((window * slots, slots), jnp.float32),
            jax.ShapeDtypeStruct((slots, 1), jnp.float32),
            jax.ShapeDtypeStruct((2,), jnp.int32),
        ],
        compiler_params=pltpu.CompilerParams(vmem_limit_bytes=VMEM_BYTES),
        name="prepare_rows",
    )(band_counts, latent, gain)


def gather_kernel(
    bands,
    window,
    normed_ref,
    wq_ref,
    wk_ref,
    wv_ref,
    q_ref,
    k_ref,
    v_ref,
    held,
    send_sem,
    recv_sem,
    pass_send,
    pass_recv,
):
    member, band, pair, core = band_layout()
    pairs = bands // 2
    slots = normed_ref.shape[0]
    sibling = (member, 2 * pair + 1 - core)
    order = far_first(pairs)
    targets = {d: (member, 2 * partner(pair, d) + core) for d in order}
    greet([sibling] + [targets[d] for d in order])
    own = pl.ds(pl.multiple_of(band * slots, slots), slots)
    copies = {
        d: send(normed_ref, held.at[own], send_sem.at[d], recv_sem.at[d], targets[d])
        for d in order
    }
    copies[0] = send(normed_ref, held.at[own], send_sem.at[0], recv_sem.at[0], sibling)
    for d in [0] + order[::-1]:
        copies[d].start()
    first = jnp.clip(band - HOPS, 0, bands - window)

    def project(source, count):
        rows = pl.ds(pl.multiple_of(source * slots, slots), count * slots)
        place = pl.ds(pl.multiple_of((source - first) * slots, slots), count * slots)
        project_into(held.at[rows], wk_ref, k_ref.at[place])
        project_into(held.at[rows], wv_ref, v_ref.at[place])

    def project_pair(source_pair):
        if window == bands:
            project(2 * source_pair, 2)
        else:
            for source in (2 * source_pair, 2 * source_pair + 1):
                inside = (source >= first) & (source < first + window)
                pl.when(inside)(functools.partial(project, source, 1))

    held[own, :] = normed_ref[...]
    project_into(normed_ref, wq_ref, q_ref)
    copies[0].wait_recv()
    project_pair(pair)
    passes = {}
    for d in order[::-1]:
        copies[d].wait_recv()
        source = 2 * partner(pair, d) + core
        rows = pl.ds(pl.multiple_of(source * slots, slots), slots)
        passes[d] = send(held.at[rows], held.at[rows], pass_send.at[d], pass_recv.at[d], sibling)
        passes[d].start()
        passes[d].wait_recv()
        project_pair(partner(pair, d))
    for d in order + [0]:
        copies[d].wait_send()
    for d in order:
        passes[d].wait_send()


def gather_and_project(normed, w_query, w_key, w_value, bands, window):
    slots, model_width = normed.shape
    vmem = pl.BlockSpec(memory_space=pltpu.VMEM)
    pairs = bands // 2
    return pl.pallas_call(
        functools.partial(gather_kernel, bands, window),
        in_specs=[vmem] * 4,
        out_specs=[vmem] * 3,
        out_shape=[
            jax.ShapeDtypeStruct((slots, model_width), jnp.bfloat16),
            jax.ShapeDtypeStruct((window * slots, model_width), jnp.bfloat16),
            jax.ShapeDtypeStruct((window * slots, model_width), jnp.bfloat16),
        ],
        scratch_shapes=[
            pltpu.VMEM((bands * slots, model_width), jnp.bfloat16),
            pltpu.SemaphoreType.DMA((pairs,)),
            pltpu.SemaphoreType.DMA((pairs,)),
            pltpu.SemaphoreType.DMA((pairs,)),
            pltpu.SemaphoreType.DMA((pairs,)),
        ],
        compiler_params=pltpu.CompilerParams(
            collective_id=0, has_side_effects=True, vmem_limit_bytes=VMEM_BYTES
        ),
        name="gather_rows",
    )(normed, w_query, w_key, w_value)


def member_targets(members):
    member = lax.axis_index("member")
    band = lax.axis_index("band")
    return [(lax.rem(member + d, members), band) for d in range(1, members)]


def exchange_kernel(members, own_ref, all_ref, held, send_sem, recv_sem):
    targets = member_targets(members)
    greet(targets)
    copies = [
        send(own_ref, held.at[d], send_sem.at[d], recv_sem.at[d], targets[d])
        for d in range(members - 1)
    ]
    for copy in copies:
        copy.start()
    for d, copy in enumerate(copies):
        copy.wait_recv()
        all_ref[d] = held[d]
    for copy in copies:
        copy.wait_send()


def exchange_members(own, members):
    vmem = pl.BlockSpec(memory_space=pltpu.VMEM)
    return pl.pallas_call(
        functools.partial(exchange_kernel, members),
        in_specs=[vmem],
        out_specs=vmem,
        out_shape=jax.ShapeDtypeStruct((members - 1,) + own.shape, own.dtype),
        scratch_shapes=[
            pltpu.VMEM((members - 1,) + own.shape, own.dtype),
            pltpu.SemaphoreType.DMA((members - 1,)),
            pltpu.SemaphoreType.DMA((members - 1,)),
        ],
        compiler_params=pltpu.CompilerParams(collective_id=1, has_side_effects=True),
        name="exchange_members",
    )(own)


def backward_kernel(
    bands,
    members,
    head_size,
    q_ref,
    k_ref,
    v_ref,
    up_ref,
    mixed_ref,
    lse_ref,
    bias_ref,
    wk_ref,
    wv_ref,
    head_ref,
    dq_ref,
    total_ref,
    head_out,
    dq_sum,
    query_held,
    up_held,
    inner_held,
    dk_held,
    dv_held,
    for_sibling,
    from_sibling,
    outgoing,
    arriving,
    head_bands,
    head_own,
    head_members,
    sib_send,
    sib_recv,
    far_send,
    far_recv,
    band_send,
    band_recv,
    head_send,
    head_recv,
):
    member, band, pair, core = band_layout()
    pairs = bands // 2
    slots = total_ref.shape[0]
    window = k_ref.shape[0] // slots
    steps = q_ref.shape[1] // LANES
    heads = LANES // head_size
    scale = 1.0 / math.sqrt(head_size)
    sibling = (member, 2 * pair + 1 - core)
    order = far_first(pairs)
    targets = {d: (member, 2 * partner(pair, d) + core) for d in order}
    others = member_targets(members)
    ring = [lax.rem(band + d, bands) for d in range(1, bands)]
    greet([(member, other) for other in ring] + others)
    band_copies = [
        send(
            head_ref.at[other],
            head_bands.at[band],
            band_send.at[d],
            band_recv.at[d],
            (member, other),
        )
        for d, other in enumerate(ring)
    ]
    for copy in band_copies:
        copy.start()
    head_bands[band] = head_ref[band]
    first = jnp.clip(band - HOPS, 0, bands - window)
    masks = head_masks((slots, LANES), 1, heads, head_size)

    @pl.loop(0, steps)
    def _(i):
        lanes = pl.ds(pl.multiple_of(i * LANES, LANES), LANES)
        up = up_ref[:, lanes]
        product = (up.astype(jnp.float32) * mixed_ref[:, lanes]).T
        query_heads = masked_heads(q_ref[:, lanes], masks, scale)
        up_heads = masked_heads(up, masks, 1.0)
        for h in range(heads):
            query_held[i, h] = query_heads[h]
            up_held[i, h] = up_heads[h]
            inner_held[i, h : h + 1, :] = jnp.sum(
                product[h * head_size : (h + 1) * head_size], axis=0, keepdims=True
            )
        dq_sum[i] = jnp.zeros((LANES, slots), jnp.float32)

    def terms_of(target, out_ref):
        inside = (target - band <= HOPS) & (band - target <= HOPS)

        @pl.when(inside)
        def _():
            place = pl.ds(pl.multiple_of((target - first) * slots, slots), slots)

            @pl.loop(0, steps)
            def _(i):
                lanes = pl.ds(pl.multiple_of(i * LANES, LANES), LANES)
                keys = k_ref[place, lanes]
                values = v_ref[place, lanes]
                bias = bias_ref[place, :]
                key_sum = jnp.zeros((slots, LANES), jnp.float32)
                value_sum = jnp.zeros((slots, LANES), jnp.float32)
                for h in range(heads):
                    query = query_held[i, h]
                    up = up_held[i, h]
                    soft = jnp.exp(dot_last(keys, query) + (bias - lse_ref[i, h : h + 1, :]))
                    d_soft = dot_last(values, up)
                    d_score = (soft * (d_soft - inner_held[i, h : h + 1, :])).astype(jnp.bfloat16)
                    key_sum += jnp.dot(d_score, query, preferred_element_type=jnp.float32)
                    value_sum += jnp.dot(
                        soft.astype(jnp.bfloat16), up, preferred_element_type=jnp.float32
                    )
                    part = pl.ds(h * head_size, head_size)
                    dq_sum[i, part, :] += dot_first(keys, d_score)[
                        h * head_size : (h + 1) * head_size
                    ]
                dk_held[:, lanes] = key_sum.astype(jnp.bfloat16)
                dv_held[:, lanes] = value_sum.astype(jnp.bfloat16)

            @pl.loop(0, wk_ref.shape[0] // COLUMNS)
            def _(tile):
                at = pl.ds(pl.multiple_of(tile * COLUMNS, COLUMNS), COLUMNS)
                out_ref[:, at] = (
                    dot_last(dk_held[...], wk_ref[at, :]) + dot_last(dv_held[...], wv_ref[at, :])
                ).astype(out_ref.dtype)

        @pl.when(jnp.logical_not(inside))
        def _():
            out_ref[...] = jnp.zeros(out_ref.shape, out_ref.dtype)

    near = {}
    far = {}
    for d in order + [0]:
        there = partner(pair, d)
        terms_of(2 * there + 1 - core, for_sibling.at[d])
        near[d] = send(
            for_sibling.at[d], from_sibling.at[d], sib_send.at[d], sib_recv.at[d], sibling
        )
        near[d].start()
        terms_of(2 * there + core, outgoing.at[d])
        near[d].wait_recv()
        if d:
            outgoing[d] = (
                outgoing[d].astype(jnp.float32) + from_sibling[d].astype(jnp.float32)
            ).astype(jnp.bfloat16)
            far[d] = send(
                outgoing.at[d], arriving.at[d], far_send.at[d], far_recv.at[d], targets[d]
            )
            far[d].start()
        else:
            total_ref[...] = outgoing[0].astype(jnp.float32) + from_sibling[0].astype(jnp.float32)
        if d == order[-1]:
            for copy in band_copies:
                copy.wait_recv()
            head_sum = head_bands[0]
            for other in range(1, bands):
                head_sum += head_bands[other]
            head_own[...] = head_sum
            head_copies = [
                send(
                    head_own, head_members.at[member], head_send.at[e], head_recv.at[e], others[e]
                )
                for e in range(members - 1)
            ]
            for copy in head_copies:
                copy.start()
            head_members[member] = head_sum

    @pl.loop(0, steps)
    def _(i):
        lanes = pl.ds(pl.multiple_of(i * LANES, LANES), LANES)
        dq_ref[:, lanes] = (dq_sum[i] * scale).T.astype(jnp.bfloat16)

    for copy in head_copies:
        copy.wait_recv()
    head_sum = head_members[0]
    for other in range(1, members):
        head_sum += head_members[other]
    head_out[...] = head_sum
    for d in order:
        far[d].wait_recv()
        total_ref[...] += arriving[d].astype(jnp.float32)
    for d in order:
        far[d].wait_send()
        near[d].wait_send()
    near[0].wait_send()
    for copy in band_copies + head_copies:
        copy.wait_send()


def attention_backward(
    queries, key_rows, value_rows, upstream, mixed, lse, bias, w_key, w_value, head, members
):
    slots, model_width = queries.shape
    bands, head_rows, channels = head.shape
    head_size = model_width // HEADS
    heads = LANES // head_size
    steps = model_width // LANES
    vmem = pl.BlockSpec(memory_space=pltpu.VMEM)
    pairs = bands // 2
    blocks = pltpu.VMEM((pairs, slots, model_width), jnp.bfloat16)
    rows = pltpu.VMEM((slots, model_width), jnp.bfloat16)
    masked = pltpu.VMEM((steps, heads, slots, LANES), jnp.bfloat16)
    return pl.pallas_call(
        functools.partial(backward_kernel, bands, members, head_size),
        in_specs=[vmem] * 10,
        out_specs=[vmem] * 3,
        out_shape=[
            jax.ShapeDtypeStruct((slots, model_width), jnp.bfloat16),
            jax.ShapeDtypeStruct((slots, model_width), jnp.float32),
            jax.ShapeDtypeStruct((head_rows, channels), jnp.float32),
        ],
        scratch_shapes=[
            pltpu.VMEM((steps, LANES, slots), jnp.float32),
            masked,
            masked,
            pltpu.VMEM((steps, heads, slots), jnp.float32),
            rows,
            rows,
            blocks,
            blocks,
            blocks,
            blocks,
            pltpu.VMEM((bands, head_rows, channels), jnp.float32),
            pltpu.VMEM((head_rows, channels), jnp.float32),
            pltpu.VMEM((members, head_rows, channels), jnp.float32),
            pltpu.SemaphoreType.DMA((pairs,)),
            pltpu.SemaphoreType.DMA((pairs,)),
            pltpu.SemaphoreType.DMA((pairs,)),
            pltpu.SemaphoreType.DMA((pairs,)),
            pltpu.SemaphoreType.DMA((bands - 1,)),
            pltpu.SemaphoreType.DMA((bands - 1,)),
            pltpu.SemaphoreType.DMA((members - 1,)),
            pltpu.SemaphoreType.DMA((members - 1,)),
        ],
        compiler_params=pltpu.CompilerParams(
            collective_id=2, has_side_effects=True, vmem_limit_bytes=VMEM_BYTES
        ),
        name="attention_backward",
    )(queries, key_rows, value_rows, upstream, mixed, lse, bias, w_key, w_value, head)


def own_accuracy(own, others, measured, weight):
    members = others.shape[0] + 1
    fair = 1.0 - (1.0 - FAIR_ALPHA) / members
    gap = own - measured
    smooth = jnp.sqrt(gap * gap + SMOOTH_WIDTH * SMOOTH_WIDTH)
    pair_sum = jnp.zeros_like(gap)
    slope_sum = jnp.zeros_like(gap)
    for other in range(members - 1):
        pair_gap = own - others[other]
        pair = jnp.sqrt(pair_gap * pair_gap + SMOOTH_WIDTH * SMOOTH_WIDTH)
        pair_sum += pair
        slope_sum += pair_gap / pair
    score = smooth / members - fair / (2.0 * members * (members - 1)) * pair_sum
    gradient = weight * (gap / smooth / members - fair / (members * (members - 1.0)) * slope_sum)
    return jnp.sum(weight * score), gradient


def body(
    latent,
    observed,
    area_weight,
    band_counts,
    gain_attn,
    w_query,
    w_key,
    w_value,
    w_out,
    gain_head,
    w_head,
):
    band = lax.axis_index("band")
    bands = lax.axis_size("band")
    members = lax.axis_size("member")
    _, slots, model_width = latent.shape
    channels = w_head.shape[1]
    window = min(bands, 2 * HOPS + 1)

    latent_f = latent[0].astype(jnp.float32)
    normed, bias, inverse_one, reach = prepare_rows(
        band_counts, latent[0], gain_attn[None], bands, window
    )
    queries, key_rows, value_rows = gather_and_project(
        normed, w_query, w_key, w_value, bands, window
    )
    own_live = jnp.arange(slots, dtype=jnp.int32) < band_counts[band]

    mixed, lse = attention_forward(queries, key_rows, value_rows, bias, reach)
    hidden = latent_f + jnp.dot(
        mixed.astype(jnp.bfloat16), w_out, preferred_element_type=jnp.float32
    )
    inverse_two = inverse_rms(hidden)
    head_in = (hidden * inverse_two * gain_head).astype(jnp.bfloat16)
    predicted = jnp.dot(head_in, w_head, preferred_element_type=jnp.float32).astype(jnp.bfloat16)
    others = exchange_members(predicted, members)
    total_live = jnp.sum(band_counts).astype(jnp.float32) * CH
    point_weight = area_weight * own_live.astype(jnp.float32) / total_live
    loss_part, gradient = own_accuracy(
        predicted.astype(jnp.float32),
        others.astype(jnp.float32),
        observed.astype(jnp.float32),
        point_weight[:, None],
    )
    grad_pred = gradient.astype(jnp.bfloat16)
    grad_hidden = norm_backward(hidden, gain_head, inverse_two, times_transposed(grad_pred, w_head))
    grad_mixed = times_transposed(grad_hidden.astype(jnp.bfloat16), w_out).astype(jnp.bfloat16)

    head_part = dot_first(head_in, grad_pred).reshape(bands, model_width // bands, channels)
    loss_rows = jnp.broadcast_to(loss_part, (bands, 8, channels))
    packed = jnp.concatenate([head_part, loss_rows], axis=1)
    grad_queries, normed_total, packed = attention_backward(
        queries,
        key_rows,
        value_rows,
        grad_mixed,
        mixed,
        lse,
        bias,
        w_key,
        w_value,
        packed,
        members,
    )
    grad_head = packed[: model_width // bands]
    ensemble_loss = packed[model_width // bands, 0]
    grad_normed = times_transposed(grad_queries, w_query) + normed_total
    grad_latent = (
        grad_hidden + norm_backward(latent_f, gain_attn, inverse_one, grad_normed)
    ).astype(jnp.bfloat16)
    return (grad_latent[None], grad_head, ensemble_loss)


def solution(mesh):
    placed = (
        P("member", "band", None),
        P("band", None),
        P("band"),
        P(),
        P(),
        P(),
        P(),
        P(),
        P(),
        P(),
        P(),
    )
    return jax.shard_map(
        body,
        mesh=mesh,
        in_specs=placed,
        out_specs=(P("member", "band", None), P("band", None), P()),
        check_vma=False,
    )
```

```python
import functools
import math

import jax
import jax.numpy as jnp
from jax import lax
from jax.experimental import pallas as pl
from jax.experimental.pallas import tpu as pltpu
from jax.sharding import PartitionSpec as P

HEADS = 16
CH = 128
R = 512
HOPS = 4


NORM_EPS = 1e-06
SMOOTH_WIDTH = 0.25
FAIR_ALPHA = 0.95
LANES = 128
MASKED = -1e30
VMEM_BYTES = 56 * 1024 * 1024


def inverse_rms(values):
    return lax.rsqrt(jnp.mean(values * values, axis=-1, keepdims=True) + NORM_EPS)


def norm_backward(values, gain_vec, inverse, upstream):
    scaled = upstream * gain_vec
    return inverse * scaled - values * inverse**3 * jnp.mean(
        values * scaled, axis=-1, keepdims=True
    )


def times_transposed(left_side, scaling_coefficient):
    return lax.dot_general(
        left_side,
        scaling_coefficient,
        (((left_side.ndim - 1,), (1,)), ((), ())),
        preferred_element_type=jnp.float32,
    )


def dot_last(left_side, right_side):
    return lax.dot_general(
        left_side, right_side, (((1,), (1,)), ((), ())), preferred_element_type=jnp.float32
    )


def dot_first(left_side, right_side):
    return lax.dot_general(
        left_side, right_side, (((0,), (0,)), ((), ())), preferred_element_type=jnp.float32
    )


def head_masks(shape, dimension, heads, head_size):
    lane = lax.broadcasted_iota(jnp.int32, shape, dimension)
    return [(lane >= h * head_size) & (lane < (h + 1) * head_size) for h in range(heads)]


def masked_heads(block, masks, factor):
    wide = block.astype(jnp.float32) * factor
    return [jnp.where(mask, wide, 0.0).astype(jnp.bfloat16) for mask in masks]


def forward_kernel(
    head_size, tile, reach_ref, q_ref, k_ref, v_ref, bias_ref, out_ref, lse_ref, exp_ref
):
    heads = LANES // head_size
    rows = q_ref.shape[0]
    scale = 1.0 / math.sqrt(head_size)
    masks = head_masks(q_ref.shape, 1, heads, head_size)
    query_heads = masked_heads(q_ref[...], masks, scale)

    def score_step(block, totals):
        at = pl.ds(pl.multiple_of(block * tile, tile), tile)
        keys = k_ref[at, :]
        bias = bias_ref[at, :]
        new = []
        for h in range(heads):
            weight = jnp.exp(dot_last(keys, query_heads[h]) + bias)
            exp_ref[h, at, :] = weight
            new.append(totals[h] + jnp.sum(weight.reshape(tile // 8, 8, rows), axis=0))
        return tuple(new)

    zero = tuple(jnp.zeros((8, rows), jnp.float32) for _ in range(heads))
    partial = lax.fori_loop(reach_ref[0], reach_ref[1], score_step, zero)
    totals = [jnp.sum(part, axis=0, keepdims=True) for part in partial]
    shrink = [jnp.where(total > 1e30, 0.0625, 1.0) for total in totals]
    inverse = [1.0 / (total * small) for total, small in zip(totals, shrink)]

    def value_step(block, mixed):
        at = pl.ds(pl.multiple_of(block * tile, tile), tile)
        values = v_ref[at, :]
        return tuple(
            mixed[h] + dot_first(values, (exp_ref[h, at, :] * inverse[h]).astype(jnp.bfloat16))
            for h in range(heads)
        )

    zero = tuple(jnp.zeros((LANES, rows), jnp.float32) for _ in range(heads))
    mixed = lax.fori_loop(reach_ref[0], reach_ref[1], value_step, zero)
    columns = jnp.concatenate(
        [mixed[h][h * head_size : (h + 1) * head_size] * shrink[h] for h in range(heads)], axis=0
    )
    out_ref[...] = columns.T
    for h in range(heads):
        lse_ref[0, h : h + 1, :] = jnp.log(totals[h])


def attention_forward(queries, key_rows, value_rows, bias, reach):
    rows, model_width = queries.shape
    slots = key_rows.shape[0]
    head_size = model_width // HEADS
    heads = LANES // head_size
    steps = model_width // LANES
    return pl.pallas_call(
        functools.partial(forward_kernel, head_size, rows),
        grid=(steps,),
        in_specs=[
            pl.BlockSpec(memory_space=pltpu.SMEM),
            pl.BlockSpec((rows, LANES), lambda i: (0, i)),
            pl.BlockSpec((slots, LANES), lambda i: (0, i)),
            pl.BlockSpec((slots, LANES), lambda i: (0, i)),
            pl.BlockSpec((slots, rows), lambda i: (0, 0)),
        ],
        out_specs=[
            pl.BlockSpec((rows, LANES), lambda i: (0, i)),
            pl.BlockSpec((1, heads, rows), lambda i: (i, 0, 0)),
        ],
        out_shape=[
            jax.ShapeDtypeStruct((rows, model_width), jnp.float32),
            jax.ShapeDtypeStruct((steps, heads, rows), jnp.float32),
        ],
        scratch_shapes=[pltpu.VMEM((heads, slots, rows), jnp.float32)],
        compiler_params=pltpu.CompilerParams(vmem_limit_bytes=VMEM_BYTES),
        name="attention_forward",
    )(reach, queries, key_rows, value_rows, bias)


MESH = pl.DeviceIdType.MESH
COLUMNS = 256


def partner(index, distance):
    bit = 1
    flipped = index
    while bit <= distance:
        if distance & bit:
            flipped = flipped + (1 - 2 * ((index // bit) % 2)) * bit
        bit *= 2
    return flipped


def band_layout():
    band = lax.axis_index("band")
    return lax.axis_index("member"), band, band // 2, band % 2


def far_first(pairs):
    return sorted(range(1, pairs), key=lambda d: (-bin(d).count("1"), d))


def greet(targets):
    barrier = pltpu.get_barrier_semaphore()
    for target in targets:
        pl.semaphore_signal(barrier, inc=1, device_id=target, device_id_type=MESH)
    pl.semaphore_wait(barrier, len(targets))


def send(source, target_ref, send_sem, recv_sem, target):
    return pltpu.make_async_remote_copy(
        src_ref=source,
        dst_ref=target_ref,
        send_sem=send_sem,
        recv_sem=recv_sem,
        device_id=target,
        device_id_type=MESH,
    )


def project_into(rows_ref, weight_ref, out_ref):
    @pl.loop(0, weight_ref.shape[1] // COLUMNS)
    def _(tile):
        at = pl.ds(pl.multiple_of(tile * COLUMNS, COLUMNS), COLUMNS)
        out_ref[:, at] = jnp.dot(
            rows_ref[...], weight_ref[:, at], preferred_element_type=jnp.float32
        ).astype(out_ref.dtype)


def write_mask(bands, window, band, first, slots, counts_ref, bias_ref, reach_ref):
    own_first = jnp.int32(0)
    start = jnp.int32(0)
    for b in range(bands):
        own_first += jnp.where(b < band, counts_ref[b], 0)
        start += jnp.where(b < first, counts_ref[b], 0)
    key_slot = lax.broadcasted_iota(jnp.int32, (slots, slots), 0)
    query_slot = lax.broadcasted_iota(jnp.int32, (slots, slots), 1)

    def one_band(w, carry):
        low, high, start = carry
        count = counts_ref[first + w]
        within = jnp.abs(first + w - band) <= HOPS
        live = key_slot < jnp.where(within, count, 0)
        gap = (key_slot - query_slot) + (start - own_first)
        place = pl.ds(pl.multiple_of(w * slots, slots), slots)
        bias_ref[place, :] = jnp.where(live & (jnp.abs(gap) <= R), 0.0, MASKED)
        reached = (
            within
            & (start <= own_first + (slots - 1) + R)
            & (start + count - 1 >= own_first - R)
        )
        low = jnp.minimum(low, jnp.where(reached, w, window))
        high = jnp.maximum(high, jnp.where(reached, w + 1, 0))
        return low, high, start + count

    low, high, _ = lax.fori_loop(
        0, window, one_band, (jnp.int32(window), jnp.int32(0), start)
    )
    reach_ref[0] = low
    reach_ref[1] = high


def prepare_kernel(
    bands,
    window,
    counts_ref,
    latent_ref,
    gain_ref,
    normed_ref,
    bias_ref,
    inverse_ref,
    share_ref,
    reach_ref,
):
    band = lax.axis_index("band")
    first = jnp.clip(band - HOPS, 0, bands - window)
    latent = latent_ref[...].astype(jnp.float32)
    inverse = inverse_rms(latent)
    inverse_ref[...] = inverse
    normed_ref[...] = (latent * inverse * gain_ref[...]).astype(jnp.bfloat16)
    total = counts_ref[0]
    for b in range(1, bands):
        total += counts_ref[b]
    slot = lax.broadcasted_iota(jnp.int32, share_ref.shape, 0)
    all_points = jnp.full(share_ref.shape, total, jnp.int32).astype(jnp.float32) * CH
    share_ref[...] = jnp.where(slot < counts_ref[band], 1.0, 0.0) / all_points
    write_mask(bands, window, band, first, latent.shape[0], counts_ref, bias_ref, reach_ref)


def prepare_rows(band_counts, latent, gain, bands, window):
    slots, model_width = latent.shape
    vmem = pl.BlockSpec(memory_space=pltpu.VMEM)
    smem = pl.BlockSpec(memory_space=pltpu.SMEM)
    return pl.pallas_call(
        functools.partial(prepare_kernel, bands, window),
        in_specs=[smem, vmem, vmem],
        out_specs=[vmem, vmem, vmem, vmem, smem],
        out_shape=[
            jax.ShapeDtypeStruct((slots, model_width), jnp.bfloat16),
            jax.ShapeDtypeStruct((window * slots, slots), jnp.float32),
            jax.ShapeDtypeStruct((slots, 1), jnp.float32),
            jax.ShapeDtypeStruct((slots, 1), jnp.float32),
            jax.ShapeDtypeStruct((2,), jnp.int32),
        ],
        compiler_params=pltpu.CompilerParams(vmem_limit_bytes=VMEM_BYTES),
        name="prepare_rows",
    )(band_counts, latent, gain)


def gather_kernel(
    bands,
    window,
    normed_ref,
    wq_ref,
    wk_ref,
    wv_ref,
    q_ref,
    k_ref,
    v_ref,
    held,
    send_sem,
    recv_sem,
    pass_send,
    pass_recv,
):
    member, band, pair, core = band_layout()
    pairs = bands // 2
    slots = normed_ref.shape[0]
    sibling = (member, 2 * pair + 1 - core)
    order = far_first(pairs)
    targets = {d: (member, 2 * partner(pair, d) + core) for d in order}
    greet([sibling] + [targets[d] for d in order])
    own = pl.ds(pl.multiple_of(band * slots, slots), slots)
    copies = {
        d: send(normed_ref, held.at[own], send_sem.at[d], recv_sem.at[d], targets[d])
        for d in order
    }
    copies[0] = send(normed_ref, held.at[own], send_sem.at[0], recv_sem.at[0], sibling)
    for d in [0] + order[::-1]:
        copies[d].start()
    first = jnp.clip(band - HOPS, 0, bands - window)

    def project(source, count):
        rows = pl.ds(pl.multiple_of(source * slots, slots), count * slots)
        place = pl.ds(pl.multiple_of((source - first) * slots, slots), count * slots)
        project_into(held.at[rows], wk_ref, k_ref.at[place])
        project_into(held.at[rows], wv_ref, v_ref.at[place])

    def project_pair(source_pair):
        if window == bands:
            project(2 * source_pair, 2)
        else:
            for source in (2 * source_pair, 2 * source_pair + 1):
                inside = (source >= first) & (source < first + window)
                pl.when(inside)(functools.partial(project, source, 1))

    held[own, :] = normed_ref[...]
    project_into(normed_ref, wq_ref, q_ref)
    copies[0].wait_recv()
    project_pair(pair)
    passes = {}
    for d in order[::-1]:
        copies[d].wait_recv()
        source = 2 * partner(pair, d) + core
        rows = pl.ds(pl.multiple_of(source * slots, slots), slots)
        passes[d] = send(held.at[rows], held.at[rows], pass_send.at[d], pass_recv.at[d], sibling)
        passes[d].start()
        passes[d].wait_recv()
        project_pair(partner(pair, d))
    for d in order + [0]:
        copies[d].wait_send()
    for d in order:
        passes[d].wait_send()


def gather_and_project(normed, w_query, w_key, w_value, bands, window):
    slots, model_width = normed.shape
    vmem = pl.BlockSpec(memory_space=pltpu.VMEM)
    pairs = bands // 2
    return pl.pallas_call(
        functools.partial(gather_kernel, bands, window),
        in_specs=[vmem] * 4,
        out_specs=[vmem] * 3,
        out_shape=[
            jax.ShapeDtypeStruct((slots, model_width), jnp.bfloat16),
            jax.ShapeDtypeStruct((window * slots, model_width), jnp.bfloat16),
            jax.ShapeDtypeStruct((window * slots, model_width), jnp.bfloat16),
        ],
        scratch_shapes=[
            pltpu.VMEM((bands * slots, model_width), jnp.bfloat16),
            pltpu.SemaphoreType.DMA((pairs,)),
            pltpu.SemaphoreType.DMA((pairs,)),
            pltpu.SemaphoreType.DMA((pairs,)),
            pltpu.SemaphoreType.DMA((pairs,)),
        ],
        compiler_params=pltpu.CompilerParams(
            collective_id=0, has_side_effects=True, vmem_limit_bytes=VMEM_BYTES
        ),
        name="gather_rows",
    )(normed, w_query, w_key, w_value)


def member_targets(members):
    member = lax.axis_index("member")
    band = lax.axis_index("band")
    return [(lax.rem(member + d, members), band) for d in range(1, members)]


def exchange_kernel(members, own_ref, all_ref, held, send_sem, recv_sem):
    targets = member_targets(members)
    greet(targets)
    copies = [
        send(own_ref, held.at[d], send_sem.at[d], recv_sem.at[d], targets[d])
        for d in range(members - 1)
    ]
    for copy in copies:
        copy.start()
    for d, copy in enumerate(copies):
        copy.wait_recv()
        all_ref[d] = held[d]
    for copy in copies:
        copy.wait_send()


def exchange_members(own, members):
    vmem = pl.BlockSpec(memory_space=pltpu.VMEM)
    return pl.pallas_call(
        functools.partial(exchange_kernel, members),
        in_specs=[vmem],
        out_specs=vmem,
        out_shape=jax.ShapeDtypeStruct((members - 1,) + own.shape, own.dtype),
        scratch_shapes=[
            pltpu.VMEM((members - 1,) + own.shape, own.dtype),
            pltpu.SemaphoreType.DMA((members - 1,)),
            pltpu.SemaphoreType.DMA((members - 1,)),
        ],
        compiler_params=pltpu.CompilerParams(collective_id=1, has_side_effects=True),
        name="exchange_members",
    )(own)


def backward_kernel(
    bands,
    members,
    head_size,
    q_ref,
    k_ref,
    v_ref,
    up_ref,
    mixed_ref,
    lse_ref,
    bias_ref,
    wk_ref,
    wv_ref,
    head_ref,
    dq_ref,
    total_ref,
    head_out,
    dq_sum,
    query_held,
    up_held,
    inner_held,
    dk_held,
    dv_held,
    for_sibling,
    from_sibling,
    outgoing,
    arriving,
    head_bands,
    head_own,
    head_members,
    sib_send,
    sib_recv,
    far_send,
    far_recv,
    band_send,
    band_recv,
    head_send,
    head_recv,
):
    member, band, pair, core = band_layout()
    pairs = bands // 2
    slots = total_ref.shape[0]
    window = k_ref.shape[0] // slots
    steps = q_ref.shape[1] // LANES
    heads = LANES // head_size
    scale = 1.0 / math.sqrt(head_size)
    sibling = (member, 2 * pair + 1 - core)
    order = far_first(pairs)
    targets = {d: (member, 2 * partner(pair, d) + core) for d in order}
    others = member_targets(members)
    ring = [lax.rem(band + d, bands) for d in range(1, bands)]
    greet([(member, other) for other in ring] + others)
    band_copies = [
        send(
            head_ref.at[other],
            head_bands.at[band],
            band_send.at[d],
            band_recv.at[d],
            (member, other),
        )
        for d, other in enumerate(ring)
    ]
    for copy in band_copies:
        copy.start()
    head_bands[band] = head_ref[band]
    first = jnp.clip(band - HOPS, 0, bands - window)
    masks = head_masks((slots, LANES), 1, heads, head_size)

    @pl.loop(0, steps)
    def _(i):
        lanes = pl.ds(pl.multiple_of(i * LANES, LANES), LANES)
        up = up_ref[:, lanes]
        product = (up.astype(jnp.float32) * mixed_ref[:, lanes]).T
        query_heads = masked_heads(q_ref[:, lanes], masks, scale)
        up_heads = masked_heads(up, masks, 1.0)
        for h in range(heads):
            query_held[i, h] = query_heads[h]
            up_held[i, h] = up_heads[h]
            inner_held[i, h : h + 1, :] = jnp.sum(
                product[h * head_size : (h + 1) * head_size], axis=0, keepdims=True
            )
        dq_sum[i] = jnp.zeros((LANES, slots), jnp.float32)

    def terms_of(target, out_ref):
        inside = (target - band <= HOPS) & (band - target <= HOPS)

        @pl.when(inside)
        def _():
            place = pl.ds(pl.multiple_of((target - first) * slots, slots), slots)

            @pl.loop(0, steps)
            def _(i):
                lanes = pl.ds(pl.multiple_of(i * LANES, LANES), LANES)
                keys = k_ref[place, lanes]
                values = v_ref[place, lanes]
                bias = bias_ref[place, :]
                key_sum = jnp.zeros((slots, LANES), jnp.float32)
                value_sum = jnp.zeros((slots, LANES), jnp.float32)
                for h in range(heads):
                    query = query_held[i, h]
                    up = up_held[i, h]
                    soft = jnp.exp(dot_last(keys, query) + (bias - lse_ref[i, h : h + 1, :]))
                    d_soft = dot_last(values, up)
                    d_score = (soft * (d_soft - inner_held[i, h : h + 1, :])).astype(jnp.bfloat16)
                    key_sum += jnp.dot(d_score, query, preferred_element_type=jnp.float32)
                    value_sum += jnp.dot(
                        soft.astype(jnp.bfloat16), up, preferred_element_type=jnp.float32
                    )
                    part = pl.ds(h * head_size, head_size)
                    dq_sum[i, part, :] += dot_first(keys, d_score)[
                        h * head_size : (h + 1) * head_size
                    ]
                dk_held[:, lanes] = key_sum.astype(jnp.bfloat16)
                dv_held[:, lanes] = value_sum.astype(jnp.bfloat16)

            @pl.loop(0, wk_ref.shape[0] // COLUMNS)
            def _(tile):
                at = pl.ds(pl.multiple_of(tile * COLUMNS, COLUMNS), COLUMNS)
                out_ref[:, at] = (
                    dot_last(dk_held[...], wk_ref[at, :]) + dot_last(dv_held[...], wv_ref[at, :])
                ).astype(out_ref.dtype)

        @pl.when(jnp.logical_not(inside))
        def _():
            out_ref[...] = jnp.zeros(out_ref.shape, out_ref.dtype)

    near = {}
    far = {}
    for d in order + [0]:
        there = partner(pair, d)
        terms_of(2 * there + 1 - core, for_sibling.at[d])
        near[d] = send(
            for_sibling.at[d], from_sibling.at[d], sib_send.at[d], sib_recv.at[d], sibling
        )
        near[d].start()
        terms_of(2 * there + core, outgoing.at[d])
        near[d].wait_recv()
        if d:
            outgoing[d] = (
                outgoing[d].astype(jnp.float32) + from_sibling[d].astype(jnp.float32)
            ).astype(jnp.bfloat16)
            far[d] = send(
                outgoing.at[d], arriving.at[d], far_send.at[d], far_recv.at[d], targets[d]
            )
            far[d].start()
        else:
            total_ref[...] = outgoing[0].astype(jnp.float32) + from_sibling[0].astype(jnp.float32)
        if d == order[-1]:
            for copy in band_copies:
                copy.wait_recv()
            head_sum = head_bands[0]
            for other in range(1, bands):
                head_sum += head_bands[other]
            head_own[...] = head_sum
            head_copies = [
                send(
                    head_own, head_members.at[member], head_send.at[e], head_recv.at[e], others[e]
                )
                for e in range(members - 1)
            ]
            for copy in head_copies:
                copy.start()
            head_members[member] = head_sum

    @pl.loop(0, steps)
    def _(i):
        lanes = pl.ds(pl.multiple_of(i * LANES, LANES), LANES)
        dq_ref[:, lanes] = (dq_sum[i] * scale).T.astype(jnp.bfloat16)

    for copy in head_copies:
        copy.wait_recv()
    head_sum = head_members[0]
    for other in range(1, members):
        head_sum += head_members[other]
    head_out[...] = head_sum
    for d in order:
        far[d].wait_recv()
        total_ref[...] += arriving[d].astype(jnp.float32)
    for d in order:
        far[d].wait_send()
        near[d].wait_send()
    near[0].wait_send()
    for copy in band_copies + head_copies:
        copy.wait_send()


def attention_backward(
    queries, key_rows, value_rows, upstream, mixed, lse, bias, w_key, w_value, head, members
):
    slots, model_width = queries.shape
    bands, head_rows, channels = head.shape
    head_size = model_width // HEADS
    heads = LANES // head_size
    steps = model_width // LANES
    vmem = pl.BlockSpec(memory_space=pltpu.VMEM)
    pairs = bands // 2
    blocks = pltpu.VMEM((pairs, slots, model_width), jnp.bfloat16)
    rows = pltpu.VMEM((slots, model_width), jnp.bfloat16)
    masked = pltpu.VMEM((steps, heads, slots, LANES), jnp.bfloat16)
    return pl.pallas_call(
        functools.partial(backward_kernel, bands, members, head_size),
        in_specs=[vmem] * 10,
        out_specs=[vmem] * 3,
        out_shape=[
            jax.ShapeDtypeStruct((slots, model_width), jnp.bfloat16),
            jax.ShapeDtypeStruct((slots, model_width), jnp.float32),
            jax.ShapeDtypeStruct((head_rows, channels), jnp.float32),
        ],
        scratch_shapes=[
            pltpu.VMEM((steps, LANES, slots), jnp.float32),
            masked,
            masked,
            pltpu.VMEM((steps, heads, slots), jnp.float32),
            rows,
            rows,
            blocks,
            blocks,
            blocks,
            blocks,
            pltpu.VMEM((bands, head_rows, channels), jnp.float32),
            pltpu.VMEM((head_rows, channels), jnp.float32),
            pltpu.VMEM((members, head_rows, channels), jnp.float32),
            pltpu.SemaphoreType.DMA((pairs,)),
            pltpu.SemaphoreType.DMA((pairs,)),
            pltpu.SemaphoreType.DMA((pairs,)),
            pltpu.SemaphoreType.DMA((pairs,)),
            pltpu.SemaphoreType.DMA((bands - 1,)),
            pltpu.SemaphoreType.DMA((bands - 1,)),
            pltpu.SemaphoreType.DMA((members - 1,)),
            pltpu.SemaphoreType.DMA((members - 1,)),
        ],
        compiler_params=pltpu.CompilerParams(
            collective_id=2, has_side_effects=True, vmem_limit_bytes=VMEM_BYTES
        ),
        name="attention_backward",
    )(queries, key_rows, value_rows, upstream, mixed, lse, bias, w_key, w_value, head)


def own_accuracy(own, others, measured, weight):
    members = others.shape[0] + 1
    fair = 1.0 - (1.0 - FAIR_ALPHA) / members
    gap = own - measured
    smooth = jnp.sqrt(gap * gap + SMOOTH_WIDTH * SMOOTH_WIDTH)
    pair_sum = jnp.zeros_like(gap)
    slope_sum = jnp.zeros_like(gap)
    for other in range(members - 1):
        pair_gap = own - others[other]
        pair = jnp.sqrt(pair_gap * pair_gap + SMOOTH_WIDTH * SMOOTH_WIDTH)
        pair_sum += pair
        slope_sum += pair_gap / pair
    score = smooth / members - fair / (2.0 * members * (members - 1)) * pair_sum
    gradient = weight * (gap / smooth / members - fair / (members * (members - 1.0)) * slope_sum)
    return jnp.sum(weight * score), gradient


def body(
    latent,
    observed,
    area_weight,
    band_counts,
    gain_attn,
    w_query,
    w_key,
    w_value,
    w_out,
    gain_head,
    w_head,
):
    bands = lax.axis_size("band")
    members = lax.axis_size("member")
    _, slots, model_width = latent.shape
    channels = w_head.shape[1]
    window = min(bands, 2 * HOPS + 1)

    latent_f = latent[0].astype(jnp.float32)
    normed, bias, inverse_one, share, reach = prepare_rows(
        band_counts, latent[0], gain_attn[None], bands, window
    )
    queries, key_rows, value_rows = gather_and_project(
        normed, w_query, w_key, w_value, bands, window
    )
    mixed, lse = attention_forward(queries, key_rows, value_rows, bias, reach)
    hidden = latent_f + jnp.dot(
        mixed.astype(jnp.bfloat16), w_out, preferred_element_type=jnp.float32
    )
    inverse_two = inverse_rms(hidden)
    head_in = (hidden * inverse_two * gain_head).astype(jnp.bfloat16)
    predicted = jnp.dot(head_in, w_head, preferred_element_type=jnp.float32).astype(jnp.bfloat16)
    others = exchange_members(predicted, members)
    loss_part, gradient = own_accuracy(
        predicted.astype(jnp.float32),
        others.astype(jnp.float32),
        observed.astype(jnp.float32),
        area_weight[:, None] * share,
    )
    grad_pred = gradient.astype(jnp.bfloat16)
    grad_hidden = norm_backward(hidden, gain_head, inverse_two, times_transposed(grad_pred, w_head))
    grad_mixed = times_transposed(grad_hidden.astype(jnp.bfloat16), w_out).astype(jnp.bfloat16)

    head_part = dot_first(head_in, grad_pred).reshape(bands, model_width // bands, channels)
    loss_rows = jnp.broadcast_to(loss_part, (bands, 8, channels))
    packed = jnp.concatenate([head_part, loss_rows], axis=1)
    grad_queries, normed_total, packed = attention_backward(
        queries,
        key_rows,
        value_rows,
        grad_mixed,
        mixed,
        lse,
        bias,
        w_key,
        w_value,
        packed,
        members,
    )
    grad_head = packed[: model_width // bands]
    ensemble_loss = packed[model_width // bands, 0]
    grad_normed = times_transposed(grad_queries, w_query) + normed_total
    grad_latent = (
        grad_hidden + norm_backward(latent_f, gain_attn, inverse_one, grad_normed)
    ).astype(jnp.bfloat16)
    return (grad_latent[None], grad_head, ensemble_loss)


def solution(mesh):
    placed = (
        P("member", "band", None),
        P("band", None),
        P("band"),
        P(),
        P(),
        P(),
        P(),
        P(),
        P(),
        P(),
        P(),
    )
    return jax.shard_map(
        body,
        mesh=mesh,
        in_specs=placed,
        out_specs=(P("member", "band", None), P("band", None), P()),
        check_vma=False,
    )
```
